256 devices in a mesh: dp: 16 (over z, core), rank: 16 (over x, y).
Axes of the slice: x: 4, y: 4, z: 8, core: 2. Of those that a mesh axis runs over, the one named last changes fastest.
Arguments:
- grad_parts: bfloat16 [16, 4096, 14336], P('dp', None, 'rank'), may hold values from -3 to 3
- old_basis: bfloat16 [4096, 512], P('dp'), may hold values from -0.09375 to 0.09375
- moment_one: float32 [512, 14336], P('dp', 'rank'), may hold values from -6 to 6
- moment_two: float32 [512, 14336], P('dp', 'rank'), may hold values from 0.5 to 4
Outputs:
- new_basis: bfloat16 [4096, 512], P('dp')
- moment_new: float32 [512, 14336], P('dp', 'rank')
- second_new: float32 [512, 14336], P('dp', 'rank')
- weight_step: bfloat16 [4096, 14336], P('dp', 'rank')
The draws below stay inside these ranges and needn't reach their ends.
All inputs are finite; a program needn't handle non-finite values.
Results may differ from the reference program's by a relative error of at most 0.023.
Values may be sent and summed in bfloat16 or wider, within the bound.
No kernel may reach another device: no remote copies, remote signals or barrier semaphores. Data moves between devices by JAX's collectives and lax.ppermute only.
A program may use at most 64 MiB of HBM per device.

```python
import math
import jax
import jax.numpy as jnp
from jax import lax

D_MODEL = 4096
HIDDEN_SIZE = 14336
RANK = 512
N_DP = 16


def draw_grad_parts(key, part):
    key = jax.random.fold_in(key, 11)
    key_noise, key_shift = jax.random.split(key, 2)
    shape = (N_DP, D_MODEL, HIDDEN_SIZE)
    shift = jax.random.randint(key_shift, (), 0, N_DP)
    part_index = jax.lax.broadcasted_iota(jnp.int32, (N_DP, D_MODEL, 1), 0)
    row_block = jax.lax.broadcasted_iota(jnp.int32, (N_DP, D_MODEL, 1), 1) // (D_MODEL // N_DP)
    boost = jnp.where(row_block == (part_index + shift) % N_DP, 3.0, 1.0).astype(jnp.float32)
    values = 0.25 * jnp.clip(jax.random.normal(key_noise, shape, jnp.float32), -4.0, 4.0)
    values = jnp.clip(values * boost, -3.0, 3.0)
    return values.astype(jnp.bfloat16)


def block_scale(stream_key, extent, pieces, smallest, top_value):
    gain = 1.0
    for axis_at, shards_of in pieces:
        steps = jax.random.uniform(jax.random.fold_in(jax.random.fold_in(stream_key, 6), axis_at), (shards_of,), jnp.float32, smallest / len(pieces), top_value / len(pieces))
        gain = gain * jnp.repeat(jnp.exp(steps), extent[axis_at] // shards_of).reshape((-1,) + (1,) * (len(extent) - 1 - axis_at))
    return gain


def normal_values(rng, dims, scale, reach, shards=(), kind=jnp.bfloat16):
    gain = block_scale(rng, dims, shards, -0.22, 0.18) if shards else 1.0
    result = jax.random.normal(rng, dims, jnp.float32) * scale * gain
    return jnp.minimum(jnp.maximum(result, -reach), reach).astype(kind)


def setup_inputs(seed: int = 0) -> dict:
    keys = jax.random.split(jax.random.key(seed), 5)
    return {
        "grad_parts": draw_grad_parts(jax.random.fold_in(keys[4], 71), 0),
        "old_basis": normal_values(keys[1], (D_MODEL, RANK), D_MODEL ** -0.5, 0.09375, ((0, 16),)),
        "moment_one": normal_values(keys[2], (RANK, HIDDEN_SIZE), 1.0, 6.0, ((0, 16), (1, 16)), jnp.float32),
        "moment_two": jnp.clip(jnp.exp(math.log(4.0) - 2.0794415 * jax.random.uniform(keys[3], (RANK, HIDDEN_SIZE), jnp.float32) ** block_scale(keys[3], (RANK, HIDDEN_SIZE), ((0, 16), (1, 16)), -0.2, 0.2)), 0.5, 4.0),
    }


highest = lax.Precision.HIGHEST
beta_one = 0.9
beta_two = 0.95
eps = 1e-08

def contract_rows(left_matrix, right_matrix):
    return lax.dot_general(left_matrix.astype(jnp.float32), right_matrix.astype(jnp.float32), (((0,), (0,)), ((), ())), precision=highest, preferred_element_type=jnp.float32)

def reference(grad_parts, old_basis, moment_one, moment_two):

    def accumulate(running, partial_value):
        return (running + partial_value.astype(jnp.float32), None)
    gradient = lax.scan(accumulate, jnp.zeros(grad_parts.shape[1:], jnp.float32), grad_parts)[0]
    basis_old = old_basis.astype(jnp.float32)
    images = contract_rows(gradient, basis_old)
    sketch = jnp.dot(gradient.astype(jnp.float32), images.astype(jnp.float32), precision=highest, preferred_element_type=jnp.float32)
    gram_matrix = contract_rows(sketch, sketch)
    cosines = contract_rows(sketch, basis_old)
    factor = jnp.linalg.cholesky(gram_matrix)
    basis_exact = jax.scipy.linalg.solve_triangular(factor, sketch.T, lower=True).T
    new_basis = basis_exact.astype(jnp.bfloat16)
    rotation = jax.scipy.linalg.solve_triangular(factor, cosines, lower=True)
    projected = contract_rows(new_basis.astype(jnp.float32), gradient)
    first_rotated = jnp.dot(rotation.astype(jnp.float32), moment_one.astype(jnp.float32), precision=highest, preferred_element_type=jnp.float32)
    second_rotated = jnp.dot((rotation * rotation).astype(jnp.float32), moment_two.astype(jnp.float32), precision=highest, preferred_element_type=jnp.float32)
    moment_new = beta_one * first_rotated + (1.0 - beta_one) * projected
    second_new = beta_two * second_rotated + (1.0 - beta_two) * projected * projected
    adam_update = (moment_new / (jnp.sqrt(second_new) + eps)).astype(jnp.bfloat16)
    weight_step = jnp.dot(new_basis.astype(jnp.float32), adam_update.astype(jnp.float32), preferred_element_type=jnp.float32).astype(jnp.bfloat16)
    return (new_basis, moment_new, second_new, weight_step)
```

```python
import jax
import jax.numpy as jnp
from jax import lax
from jax.experimental import pallas as pl
from jax.experimental.pallas import tpu as pltpu
from jax.sharding import PartitionSpec as P

highest = lax.Precision.HIGHEST
beta_one = 0.9
beta_two = 0.95
eps = 1e-08
bf16 = jnp.bfloat16
f32 = jnp.float32
block_size = 128
group_size = 8

n_z = 8
n_side = 4
swap_cores = [(z * 2 + c, z * 2 + 1 - c) for z in range(n_z) for c in range(2)]
z_groups = [[z * 2 + c for z in range(n_z)] for c in range(2)]


def z_shift(step):
    return [(z * 2 + c, ((z + step) % n_z) * 2 + c) for z in range(n_z) for c in range(2)]


def x_shift(step):
    return [
        (x * n_side + y, ((x + step) % n_side) * n_side + y)
        for x in range(n_side)
        for y in range(n_side)
    ]


def y_shift(step):
    return [
        (x * n_side + y, x * n_side + (y + step) % n_side)
        for x in range(n_side)
        for y in range(n_side)
    ]


def dot_exact(left, right, dims):
    return lax.dot_general(
        left, right, (dims, ((), ())), precision=highest, preferred_element_type=f32
    )


def dot_fast(left, right, dims):
    return lax.dot_general(left, right, (dims, ((), ())), preferred_element_type=f32)


def identity(n):
    return (
        lax.broadcasted_iota(jnp.int32, (n, n), 0) == lax.broadcasted_iota(jnp.int32, (n, n), 1)
    ).astype(f32)


def inverse_of_block_factor(block):
    n = block_size
    left = block
    right = identity(n)
    finished = []
    for group in range(n // group_size):
        rows = n - group * group_size
        row_index = lax.broadcasted_iota(jnp.int32, (rows, n), 0)
        columns = []
        for j in range(group_size):
            at = group * group_size + j
            columns.append(jnp.broadcast_to(left[:, at : at + 1], (rows, n)))
        scales = []
        for j in range(group_size):
            pivot = columns[j][j : j + 1, :]
            multiplier = jnp.where(row_index > j, columns[j] * (1.0 / pivot), 0.0)
            scales.append(lax.rsqrt(pivot))
            for k in range(j + 1, group_size):
                columns[k] = columns[k] - multiplier * columns[k][j : j + 1, :]
            if group < n // group_size - 1:
                left = left - multiplier * left[j : j + 1, :]
            right = right - multiplier * right[j : j + 1, :]
        finished.append(right[:group_size, :] * jnp.concatenate(scales, axis=0))
        left = left[group_size:, :]
        right = right[group_size:, :]
    return jnp.concatenate(finished, axis=0)


def factor_kernel(gram_ref, inverse_ref, work):
    n = gram_ref.shape[0]
    work[...] = gram_ref[...]
    inverse_ref[...] = identity(n)
    for k in range(n // block_size):
        low = k * block_size
        high = low + block_size
        diagonal = inverse_of_block_factor(work[low:high, low:high])
        inverse_rows = dot_exact(diagonal, inverse_ref[low:high, :high], ((1,), (0,)))
        inverse_ref[low:high, :high] = inverse_rows
        if high < n:
            factor_rows = dot_exact(diagonal, work[low:high, high:], ((1,), (0,)))
            work[high:, high:] = work[high:, high:] - dot_exact(
                factor_rows, factor_rows, ((0,), (0,))
            )
            inverse_ref[high:, :high] = inverse_ref[high:, :high] - dot_exact(
                factor_rows, inverse_rows, ((0,), (0,))
            )


def inverse_factor(gram_matrix):
    n = gram_matrix.shape[0]
    return pl.pallas_call(
        factor_kernel,
        out_shape=jax.ShapeDtypeStruct((n, n), f32),
        scratch_shapes=[pltpu.VMEM((n, n), f32)],
        compiler_params=pltpu.CompilerParams(vmem_limit_bytes=32 * 1024 * 1024),
    )(gram_matrix)


def pick(blocks, index):
    return lax.dynamic_index_in_dim(blocks, index, 0, keepdims=False)


def sum_gradient(local_parts, z, core):
    d_model, hidden = local_parts.shape
    share = hidden // (2 * n_z)
    turned = local_parts.T.reshape(n_z, 2, share, d_model)
    other = lax.ppermute(lax.dynamic_index_in_dim(turned, 1 - core, 1, keepdims=False), "dp", swap_cores)
    keep = lax.dynamic_index_in_dim(turned, core, 1, keepdims=False)
    pair = (keep.astype(f32) + other.astype(f32)).astype(bf16)
    half = d_model // 2
    result = []
    for lanes, hops_up, hops_down in ((slice(0, half), 4, 3), (slice(half, d_model), 3, 4)):
        piece = pair[:, :, lanes]
        total = pick(piece, z).astype(f32)
        for hops, direction in ((hops_up, 1), (hops_down, -1)):
            moving = None
            for hop in range(hops, 0, -1):
                own = pick(piece, (z + direction * hop) % n_z)
                if moving is not None:
                    own = (own.astype(f32) + moving.astype(f32)).astype(bf16)
                moving = lax.ppermute(own, "dp", z_shift(direction))
            total = total + moving.astype(f32)
        result.append(total.astype(bf16))
    return jnp.concatenate(result, axis=1)


def scatter_side(blocks, shift, at):
    total = pick(blocks, at).astype(f32)
    for step in (2, 1, 3):
        arrived = lax.ppermute(pick(blocks, (at + step) % n_side), "rank", shift(step))
        total = total + arrived.astype(f32)
    return total


def gather_side(block, shift, at):
    out = jnp.zeros((n_side,) + block.shape, block.dtype)
    out = lax.dynamic_update_index_in_dim(out, block, at, 0)
    for step in (2, 1, 3):
        arrived = lax.ppermute(block, "rank", shift(step))
        out = lax.dynamic_update_index_in_dim(out, arrived, (at - step) % n_side, 0)
    return out


def on_device(grad_parts, old_basis, moment_one, moment_two):
    local_parts = grad_parts[0]
    d_model, hidden_share = local_parts.shape
    share_rows, rank = moment_one.shape[0], old_basis.shape[1]
    own = lax.axis_index("dp")
    z, core = own // 2, own % 2
    place = lax.axis_index("rank")
    x, y = place // n_side, place % n_side
    n_dp = 2 * n_z
    hidden_own = hidden_share // n_dp

    basis_all = lax.all_gather(old_basis, "dp", axis=0, tiled=True)
    moments = jnp.concatenate([moment_one, moment_two], axis=0).T
    moments = lax.all_to_all(moments, "dp", 0, 0, tiled=True)
    moments = moments.reshape(n_dp, hidden_own, 2, share_rows).transpose(2, 1, 0, 3)
    moments = moments.reshape(2, hidden_own, rank)

    gradient = sum_gradient(local_parts, z, core)
    images = dot_fast(gradient, basis_all, ((1,), (0,)))
    images_high = images.astype(bf16)
    images_low = (images - images_high.astype(f32)).astype(bf16)
    sketch_part = dot_fast(
        jnp.concatenate([gradient, gradient], axis=0),
        jnp.concatenate([images_high, images_low], axis=0),
        ((0,), (0,)),
    ).astype(bf16)

    sketch_part = sketch_part.reshape(2, d_model // 2, rank)
    arrived = lax.ppermute(pick(sketch_part, 1 - core), "dp", swap_cores)
    sketch_part = (pick(sketch_part, core).astype(f32) + arrived.astype(f32)).astype(bf16)
    rows = d_model // 2 // (n_side * n_side) // 2
    sketch_part = sketch_part.reshape(n_side, n_side, 2, rows, rank)
    first = scatter_side(sketch_part[:, :, 0], x_shift, x).astype(bf16)
    second = scatter_side(sketch_part[:, :, 1].swapaxes(0, 1), y_shift, y).astype(bf16)
    first = scatter_side(first, y_shift, y).astype(bf16)
    second = scatter_side(second, x_shift, x).astype(bf16)
    sketch_part = jnp.concatenate([first, second], axis=0)
    sketch_part = lax.all_to_all(
        sketch_part, "dp", 0, 0, tiled=True, axis_index_groups=z_groups
    ).reshape(n_z, 2 * rows // n_z, rank)
    sketch_rows = jnp.sum(sketch_part.astype(f32), axis=0).astype(bf16)

    sketch = lax.all_gather(sketch_rows, "dp", axis=0, tiled=True, axis_index_groups=z_groups)
    first, second = sketch[:rows], sketch[rows:]
    first = gather_side(first, y_shift, y)
    second = gather_side(second, x_shift, x)
    first = gather_side(first, x_shift, x)
    second = gather_side(second, y_shift, y).swapaxes(0, 1)
    sketch = jnp.stack([first, second], axis=2).reshape(d_model // 2, rank)
    arrived = lax.ppermute(sketch, "dp", swap_cores)
    sketch = jnp.where(
        core == 0,
        jnp.concatenate([sketch, arrived], axis=0),
        jnp.concatenate([arrived, sketch], axis=0),
    )

    gram_matrix = dot_fast(sketch, sketch, ((0,), (0,)))
    cosines = dot_fast(sketch, basis_all, ((0,), (0,)))
    factor_inverse = inverse_factor(gram_matrix)
    back_images = dot_fast(gradient, sketch, ((1,), (0,)))

    rotation = dot_exact(factor_inverse, cosines, ((1,), (0,)))
    sketch_own = lax.dynamic_slice_in_dim(
        sketch, own * old_basis.shape[0], old_basis.shape[0], 0
    )
    new_basis = dot_exact(sketch_own.astype(f32), factor_inverse, ((1,), (1,))).astype(bf16)
    projected = dot_exact(back_images, factor_inverse, ((1,), (1,)))
    first_rotated = dot_exact(moments[0], rotation, ((1,), (1,)))
    second_rotated = dot_exact(moments[1], rotation * rotation, ((1,), (1,)))
    moment_new = beta_one * first_rotated + (1.0 - beta_one) * projected
    second_new = beta_two * second_rotated + (1.0 - beta_two) * projected * projected
    adam_update = (moment_new / (jnp.sqrt(second_new) + eps)).astype(bf16)
    adam_all = lax.all_gather(adam_update, "dp", axis=0, tiled=True)
    weight_step = dot_fast(new_basis, adam_all, ((1,), (1,))).astype(bf16)

    back = jnp.stack([moment_new, second_new]).reshape(2, hidden_own, n_dp, share_rows)
    back = back.transpose(2, 1, 0, 3).reshape(n_dp * hidden_own, 2 * share_rows)
    back = lax.all_to_all(back, "dp", 0, 0, tiled=True).T
    return (new_basis, back[:share_rows], back[share_rows:], weight_step)


def solution(mesh):
    in_specs = (P("dp", None, "rank"), P("dp", None), P("dp", "rank"), P("dp", "rank"))
    out_specs = (P("dp", None), P("dp", "rank"), P("dp", "rank"), P("dp", "rank"))
    return jax.shard_map(
        on_device, mesh=mesh, in_specs=in_specs, out_specs=out_specs, check_vma=False
    )
```

```python
import functools
import jax
import jax.numpy as jnp
from jax import lax
from jax.experimental import pallas as pl
from jax.experimental.pallas import tpu as pltpu
from jax.sharding import PartitionSpec as P

highest = lax.Precision.HIGHEST
beta_one = 0.9
beta_two = 0.95
eps = 1e-08
bf16 = jnp.bfloat16
f32 = jnp.float32
block_size = 128
group_size = 8

n_z = 8
n_side = 4
swap_cores = [(z * 2 + c, z * 2 + 1 - c) for z in range(n_z) for c in range(2)]
z_groups = [[z * 2 + c for z in range(n_z)] for c in range(2)]
mebibyte = 1024 * 1024
tile = 128


def z_shift(step):
    return [(z * 2 + c, ((z + step) % n_z) * 2 + c) for z in range(n_z) for c in range(2)]


def z_flip(bit):
    return [(z * 2 + c, (z ^ bit) * 2 + c) for z in range(n_z) for c in range(2)]


def x_shift(step):
    return [
        (x * n_side + y, ((x + step) % n_side) * n_side + y)
        for x in range(n_side)
        for y in range(n_side)
    ]


def y_shift(step):
    return [
        (x * n_side + y, x * n_side + (y + step) % n_side)
        for x in range(n_side)
        for y in range(n_side)
    ]


def dot_exact(left, right, dims):
    return lax.dot_general(
        left, right, (dims, ((), ())), precision=highest, preferred_element_type=f32
    )


def dot_fast(left, right, dims):
    return lax.dot_general(left, right, (dims, ((), ())), preferred_element_type=f32)


def identity(n):
    return (
        lax.broadcasted_iota(jnp.int32, (n, n), 0) == lax.broadcasted_iota(jnp.int32, (n, n), 1)
    ).astype(f32)


def inverse_of_block_factor(block):
    n = block_size
    left = block
    right = identity(n)
    finished = []
    for group in range(n // group_size):
        rows = n - group * group_size
        row_index = lax.broadcasted_iota(jnp.int32, (rows, n), 0)
        columns = []
        for j in range(group_size):
            at = group * group_size + j
            columns.append(jnp.broadcast_to(left[:, at : at + 1], (rows, n)))
        scales = []
        for j in range(group_size):
            pivot = columns[j][j : j + 1, :]
            multiplier = jnp.where(row_index > j, columns[j] * (1.0 / pivot), 0.0)
            scales.append(lax.rsqrt(pivot))
            for k in range(j + 1, group_size):
                columns[k] = columns[k] - multiplier * columns[k][j : j + 1, :]
            if group < n // group_size - 1:
                left = left - multiplier * left[j : j + 1, :]
            right = right - multiplier * right[j : j + 1, :]
        finished.append(right[:group_size, :] * jnp.concatenate(scales, axis=0))
        left = left[group_size:, :]
        right = right[group_size:, :]
    return jnp.concatenate(finished, axis=0)


def eliminate_block(k, work, inverse):
    n = work.shape[0]
    low = k * block_size
    high = low + block_size
    diagonal = inverse_of_block_factor(work[low:high, low:high])
    inverse_rows = dot_exact(diagonal, inverse[low:high, :high], ((1,), (0,)))
    inverse[low:high, :high] = inverse_rows
    if high < n:
        factor_rows = dot_exact(diagonal, work[low:high, high:], ((1,), (0,)))
        work[high:, high:] = work[high:, high:] - dot_exact(factor_rows, factor_rows, ((0,), (0,)))
        inverse[high:, :high] = inverse[high:, :high] - dot_exact(
            factor_rows, inverse_rows, ((0,), (0,))
        )


def first_factor_kernel(own_ref, arrived_ref, work, inverse, token):
    token[...] = jnp.zeros_like(token)
    work[...] = own_ref[...] + arrived_ref[...]
    inverse[...] = identity(work.shape[0])
    eliminate_block(0, work, inverse)


def next_factor_kernel(k, work_in, inverse_in, token_in, work, inverse, token):
    token[...] = token_in[...]
    work[...] = work_in[...]
    inverse[...] = inverse_in[...]
    eliminate_block(k, work, inverse)


def factor_step(k, *operands):
    n = operands[0].shape[0]
    square = jax.ShapeDtypeStruct((n, n), f32)
    kernel = functools.partial(next_factor_kernel, k) if k else first_factor_kernel
    return pl.pallas_call(
        kernel,
        out_shape=(square, square, jax.ShapeDtypeStruct((8, tile), f32)),
        compiler_params=pltpu.CompilerParams(vmem_limit_bytes=12 * mebibyte),
        cost_estimate=pl.CostEstimate(flops=5 * 10**9, bytes_accessed=4 * n * n * 4, transcendentals=0),
    )(*operands)


def load_kernel(first, other_side, place_ref, parts_ref, rows_ref, semaphore):
    side = 1 - place_ref[1] if other_side else place_ref[1]
    copy = pltpu.make_async_copy(
        parts_ref.at[pl.ds(first, rows_ref.shape[0]), side], rows_ref, semaphore
    )
    copy.start()
    copy.wait()


def load_rows(blocks, place, first, other_side):
    _, _, rows, hidden = blocks.shape
    return pl.pallas_call(
        functools.partial(load_kernel, first, other_side),
        in_specs=[pl.BlockSpec(memory_space=pltpu.SMEM), pl.BlockSpec(memory_space=pltpu.HBM)],
        out_specs=pl.BlockSpec(memory_space=pltpu.VMEM),
        out_shape=jax.ShapeDtypeStruct((n_z // 2, rows, hidden), bf16),
        scratch_shapes=[pltpu.SemaphoreType.DMA],
        compiler_params=pltpu.CompilerParams(vmem_limit_bytes=8 * mebibyte),
        cost_estimate=pl.CostEstimate(flops=10**9, bytes_accessed=0, transcendentals=0),
    )(place, blocks)


def pair_kernel(place_ref, own_ref, other_ref, *refs):
    *out_refs, turned = refs
    n_blocks, rows, _ = own_ref.shape
    share = out_refs[0].shape[0]
    for block in range(n_blocks):
        total = own_ref[block].astype(f32) + other_ref[block].astype(f32)
        turned[...] = total.T.astype(bf16)
        for offset, out_ref in enumerate(out_refs):
            at = lax.rem(place_ref[0] + offset, n_z)
            chunk = turned[pl.ds(pl.multiple_of(at * share, share), share), :]
            out_ref[:, block * rows : (block + 1) * rows] = chunk


def pair_sum(place, own, other):
    n_blocks, rows, hidden = own.shape
    chunk = jax.ShapeDtypeStruct((hidden // n_z, n_blocks * rows), bf16)
    in_vmem = pl.BlockSpec(memory_space=pltpu.VMEM)
    return pl.pallas_call(
        pair_kernel,
        in_specs=[pl.BlockSpec(memory_space=pltpu.SMEM), in_vmem, in_vmem],
        out_specs=[in_vmem] * n_z,
        out_shape=[chunk] * n_z,
        scratch_shapes=[pltpu.VMEM((hidden, rows), bf16)],
        compiler_params=pltpu.CompilerParams(vmem_limit_bytes=12 * mebibyte),
        cost_estimate=pl.CostEstimate(flops=2 * 10**9, bytes_accessed=0, transcendentals=0),
    )(place, own, other)


def pick(blocks, index):
    return lax.dynamic_index_in_dim(blocks, index, 0, keepdims=False)


def swap(block):
    return lax.ppermute(block, "dp", swap_cores)


def together(*values):
    return lax.optimization_barrier(values)


def hop(up, down):
    up = lax.ppermute(up, "dp", z_shift(1))
    down = lax.ppermute(down, "dp", z_shift(-1))
    return up, down


def ring_term(own, moving):
    if moving is None:
        return own
    return (own.astype(f32) + moving.astype(f32)).astype(bf16)


def images_kernel(place_ref, *refs):
    *terms, basis_refs, gradient_ref, basis_ref, image_ref = (
        *refs[:6], refs[6 : 6 + n_z], *refs[6 + n_z :]
    )
    half = terms[0].shape[1]
    rows = basis_refs[0].shape[0]
    for side in range(2):
        own, up, down = (ref[...].astype(f32) for ref in terms[3 * side : 3 * side + 3])
        gradient_ref[:, side * half : (side + 1) * half] = (own + up + down).astype(bf16)
    for offset, ref in zip(ring_offsets, basis_refs):
        at = lax.rem(place_ref[0] + (n_z - offset), n_z)
        basis_ref[pl.ds(pl.multiple_of(at * rows, rows), rows), :] = ref[...]
    image_ref[...] = dot_fast(gradient_ref[...], basis_ref[...], ((1,), (0,)))


def sum_and_project(place, terms, basis_blocks):
    hidden, half = terms[0].shape
    rows, rank = basis_blocks[0].shape
    in_vmem = pl.BlockSpec(memory_space=pltpu.VMEM)
    return pl.pallas_call(
        images_kernel,
        in_specs=[pl.BlockSpec(memory_space=pltpu.SMEM)] + [in_vmem] * (len(terms) + n_z),
        out_shape=(
            jax.ShapeDtypeStruct((hidden, 2 * half), bf16),
            jax.ShapeDtypeStruct((n_z * rows, rank), bf16),
            jax.ShapeDtypeStruct((hidden, rank), f32),
        ),
        compiler_params=pltpu.CompilerParams(vmem_limit_bytes=16 * mebibyte),
    )(place, *terms, *basis_blocks)


def sum_gradient(local_parts, old_basis, place):
    d_model, hidden = local_parts.shape
    rows = d_model // (2 * n_z)
    blocks = local_parts.reshape(n_z, 2, rows, hidden)
    half = n_z // 2
    arrived = [swap(load_rows(blocks, place, first, True)) for first in (0, half)]
    kept_first, kept_second = [load_rows(blocks, place, first, False) for first in (0, half)]
    basis_own, kept_first = together(old_basis, kept_first)
    basis_up, basis_down = hop(basis_own, basis_own)
    pieces = [list(pair_sum(place, *pair)) for pair in zip((kept_first, kept_second), arrived)]
    basis_up, basis_down, pieces[1][0] = together(basis_up, basis_down, pieces[1][0])
    basis_blocks = [old_basis, basis_up, basis_down]

    long_up = long_down = short_up = short_down = None
    for distance in range(half, 0, -1):
        if distance > 2:
            basis_up, basis_down = hop(basis_up, basis_down)
        elif distance == 2:
            basis_up = lax.ppermute(basis_up, "dp", z_shift(1))
        long_up, long_down = hop(
            ring_term(pieces[0][distance], long_up),
            ring_term(pieces[1][-distance], long_down),
        )
        if distance > 1:
            short_up, short_down = hop(
                ring_term(pieces[1][distance - 1], short_up),
                ring_term(pieces[0][1 - distance], short_down),
            )
        if distance > 2:
            long_up, long_down, basis_up, basis_down = together(
                long_up, long_down, basis_up, basis_down
            )
            basis_blocks += [basis_up, basis_down]
        elif distance == 2:
            long_up, long_down, basis_up = together(long_up, long_down, basis_up)
            basis_blocks.append(basis_up)
        if distance > 1:
            short_up, short_down = together(short_up, short_down)
    terms = [pieces[0][0], long_up, short_down, pieces[1][0], short_up, long_down]
    return sum_and_project(place, terms, basis_blocks)


def scatter_sides(blocks, shifts, places):
    arrived = [[], []]
    for step in (2, 1, 3):
        for index, (half, shift, at) in enumerate(zip(blocks, shifts, places)):
            sent = pick(half, lax.rem(at + step, n_side))
            arrived[index].append(lax.ppermute(sent, "rank", shift(step)))
    totals = []
    for half, at, received in zip(blocks, places, arrived):
        total = pick(half, at).astype(f32)
        for block in received:
            total = total + block.astype(f32)
        totals.append(total.astype(bf16))
    return totals


def sum_blocks(blocks):
    return jnp.sum(blocks.astype(f32), axis=0).astype(bf16)


def spread_z(block):
    copies = jnp.broadcast_to(block[None], (n_z,) + block.shape)
    return lax.all_to_all(copies, "dp", 0, 0, tiled=True, axis_index_groups=z_groups)


def spread_rank(block):
    copies = jnp.broadcast_to(block[None], (lax.axis_size("rank"),) + block.shape)
    return lax.all_to_all(copies, "rank", 0, 0, tiled=True)


def split(values):
    high = values.astype(bf16)
    return high, (values - high.astype(f32)).astype(bf16)


def dot_split(left, right, dims):
    return dot_fast(left[0], right, dims) + dot_fast(left[1], right, dims)


def final_kernel(
    place_ref, inverse_ref, own_cosines_ref, other_cosines_ref, sketch_ref,
    own_moments_ref, other_moments_ref, own_back_ref, other_back_ref,
    basis_ref, moment_ref, second_ref, step_ref,
    first_in, second_in, back_in, update, moment_all, second_all,
):
    z, core = place_ref[0], place_ref[1]
    rank, hidden = first_in.shape
    share_rows = moment_ref.shape[0]
    hidden_own = hidden // (2 * n_z)
    for device_z in range(n_z):
        ring_z = lax.rem(z + (n_z - ring_offsets[device_z]), n_z)
        for side in range(2):
            mine = core == side
            device = ring_z * 2 + side
            rows = pl.ds(pl.multiple_of(device * share_rows, share_rows), share_rows)
            moments = jnp.where(mine, own_moments_ref[device_z], other_moments_ref[device_z])
            first_in[rows] = moments[:share_rows]
            second_in[rows] = moments[share_rows:]
            device = (z ^ flip_order[device_z]) * 2 + side
            rows = pl.ds(pl.multiple_of(device * hidden_own, 8), hidden_own)
            back_in[rows] = jnp.where(
                mine, own_back_ref[device_z].astype(f32), other_back_ref[device_z].astype(f32)
            )
    inverse = inverse_ref[...]
    inverse_split = split(inverse)
    sketch = sketch_ref[...]
    new_basis = (
        dot_fast(sketch, inverse_split[0], ((1,), (1,)))
        + dot_fast(sketch, inverse_split[1], ((1,), (1,)))
    ).astype(bf16)
    basis_ref[...] = new_basis
    rotation = dot_exact(inverse, own_cosines_ref[...] + other_cosines_ref[...], ((1,), (0,)))
    rotation_split = split(rotation)
    square_split = split(rotation * rotation)
    back_images = back_in[...].astype(bf16)
    step = 128
    for low in range(0, rank, step):
        rows = slice(low, low + step)
        projected = dot_split([v[rows] for v in inverse_split], back_images, ((1,), (1,)))
        first_rotated = dot_split([v[rows] for v in rotation_split], first_in[...], ((1,), (0,)))
        second_rotated = dot_split([v[rows] for v in square_split], second_in[...], ((1,), (0,)))
        moment_new = beta_one * first_rotated + (1.0 - beta_one) * projected
        second_new = beta_two * second_rotated + (1.0 - beta_two) * projected * projected
        moment_all[rows] = moment_new
        second_all[rows] = second_new
        update[rows] = (moment_new / (jnp.sqrt(second_new) + eps)).astype(bf16)
    own_rows = pl.ds(pl.multiple_of((z * 2 + core) * share_rows, share_rows), share_rows)
    moment_ref[...] = moment_all[own_rows]
    second_ref[...] = second_all[own_rows]
    step_ref[...] = dot_fast(new_basis, update[...], ((1,), (0,))).astype(bf16)


def final_step(place, inverse, cosines, sketch_own, moments, back_images):
    share_rows, hidden = moments[0].shape[1] // 2, moments[0].shape[2]
    rank = inverse.shape[0]
    rows = sketch_own.shape[0]
    in_vmem = pl.BlockSpec(memory_space=pltpu.VMEM)
    return pl.pallas_call(
        final_kernel,
        in_specs=[pl.BlockSpec(memory_space=pltpu.SMEM)] + [in_vmem] * 8,
        out_shape=(
            jax.ShapeDtypeStruct((rows, rank), bf16),
            jax.ShapeDtypeStruct((share_rows, hidden), f32),
            jax.ShapeDtypeStruct((share_rows, hidden), f32),
            jax.ShapeDtypeStruct((rows, hidden), bf16),
        ),
        scratch_shapes=[
            pltpu.VMEM((rank, hidden), bf16),
            pltpu.VMEM((rank, hidden), bf16),
            pltpu.VMEM((hidden, rank), f32),
            pltpu.VMEM((rank, hidden), bf16),
            pltpu.VMEM((rank, hidden), f32),
            pltpu.VMEM((rank, hidden), f32),
        ],
        compiler_params=pltpu.CompilerParams(vmem_limit_bytes=28 * mebibyte),
    )(place, inverse, *cosines, sketch_own, *moments, *back_images)


flip_order = (0, 4, 2, 6, 1, 5, 3, 7)

ring_offsets = (0, 1, 7, 2, 6, 3, 5, 4)


def on_device(grad_parts, old_basis, moment_one, moment_two):
    local_parts = grad_parts[0]
    d_model, hidden_share = local_parts.shape
    share_rows, rank = moment_one.shape[0], old_basis.shape[1]
    basis_rows = old_basis.shape[0]
    own = lax.axis_index("dp")
    z, core = lax.div(own, 2), lax.rem(own, 2)
    n_rank = lax.axis_size("rank")
    hidden_z = hidden_share // n_z
    moments = jnp.concatenate([moment_one, moment_two], axis=0).astype(bf16)

    place = jnp.stack([z, core]).astype(jnp.int32)
    gradient, basis_core, image_part = sum_gradient(local_parts, old_basis, place)
    images = split(image_part + swap(image_part))
    sketch_part = dot_fast(
        jnp.concatenate([gradient, gradient], axis=0), jnp.concatenate(images, axis=0), ((0,), (0,))
    ).astype(bf16)

    rows = d_model // 2 // n_rank
    place_rank = lax.axis_index("rank")
    x, y = lax.div(place_rank, n_side), lax.rem(place_rank, n_side)
    halves = sketch_part.reshape(2, n_side, n_side, rows // 2, rank)
    halves = scatter_sides((halves[0], halves[1]), (x_shift, y_shift), (x, y))
    halves = scatter_sides(halves, (y_shift, x_shift), (y, x))
    sketch_part = jnp.concatenate(halves)
    sketch_rows = sum_blocks(
        lax.all_to_all(
            sketch_part.reshape(n_z, rows // n_z, rank), "dp", 0, 0, tiled=True, axis_index_groups=z_groups
        )
    )
    sketch_rows, moments = together(sketch_rows, moments)
    up = down = moments
    gathered = [moments]
    for distance in range(n_z // 2, 0, -1):
        if distance > 1:
            up, down = hop(up, down)
            up, down = together(up, down)
            gathered += [up, down]
        else:
            gathered.append(lax.ppermute(up, "dp", z_shift(1)))
    moments = jnp.stack(gathered)
    sketch = spread_z(sketch_rows).reshape(rows, rank)
    sketch = spread_rank(sketch).reshape(n_side, n_side, 2, rows // 2, rank)
    sketch = jnp.stack([sketch[:, :, 0], sketch[:, :, 1].swapaxes(0, 1)])
    sketch = sketch.reshape(d_model // 2, rank)
    moments = (moments, swap(moments))

    back_part = dot_fast(gradient, sketch, ((1,), (0,))).reshape(2, hidden_z // 2, rank)
    back_other = swap(pick(back_part, 1 - core))
    gram_part = dot_fast(sketch, sketch, ((0,), (0,)))
    gram_other = swap(gram_part)
    cosine_part = dot_fast(sketch, basis_core, ((0,), (0,)))
    cosine_other = swap(cosine_part)

    back = (pick(back_part, core) + back_other).astype(bf16)[None]
    back = jnp.concatenate([back, lax.ppermute(back, "dp", z_flip(4))])
    *state, token = factor_step(0, gram_part, gram_other)
    for k, distance in ((1, 2), (2, 1)):
        back, token = together(back, token)
        back = jnp.concatenate([back, lax.ppermute(back, "dp", z_flip(distance))])
        *state, token = factor_step(k, *state, token)
    back, token = together(back, token)
    back = (back, swap(back))
    _, inverse, token = factor_step(3, *state, token)

    sketch_own = lax.dynamic_slice_in_dim(sketch, z * basis_rows, basis_rows, 0)
    return final_step(place, inverse, (cosine_part, cosine_other), sketch_own, moments, back)


def solution(mesh):
    in_specs = (P("dp", None, "rank"), P("dp", None), P("dp", "rank"), P("dp", "rank"))
    out_specs = (P("dp", None), P("dp", "rank"), P("dp", "rank"), P("dp", "rank"))
    return jax.shard_map(
        on_device, mesh=mesh, in_specs=in_specs, out_specs=out_specs, check_vma=False
    )
```

```python
import functools
import jax
import jax.numpy as jnp
from jax import lax
from jax.experimental import pallas as pl
from jax.experimental.pallas import tpu as pltpu
from jax.sharding import PartitionSpec as P

highest = lax.Precision.HIGHEST
beta_one = 0.9
beta_two = 0.95
eps = 1e-08
bf16 = jnp.bfloat16
f32 = jnp.float32
block_size = 128
group_size = 8

n_z = 8
swap_cores = [(z * 2 + c, z * 2 + 1 - c) for z in range(n_z) for c in range(2)]
z_groups = [[z * 2 + c for z in range(n_z)] for c in range(2)]
mebibyte = 1024 * 1024
tile = 128


def z_shift(step):
    return [(z * 2 + c, ((z + step) % n_z) * 2 + c) for z in range(n_z) for c in range(2)]


def z_flip(bit):
    return [(z * 2 + c, (z ^ bit) * 2 + c) for z in range(n_z) for c in range(2)]


def dot_exact(left, right, dims):
    return lax.dot_general(
        left, right, (dims, ((), ())), precision=highest, preferred_element_type=f32
    )


def dot_fast(left, right, dims):
    return lax.dot_general(left, right, (dims, ((), ())), preferred_element_type=f32)


def identity(n):
    return (
        lax.broadcasted_iota(jnp.int32, (n, n), 0) == lax.broadcasted_iota(jnp.int32, (n, n), 1)
    ).astype(f32)


def inverse_of_block_factor(block):
    n = block_size
    left = block
    right = identity(n)
    finished = []
    for group in range(n // group_size):
        rows = n - group * group_size
        row_index = lax.broadcasted_iota(jnp.int32, (rows, n), 0)
        columns = []
        for j in range(group_size):
            at = group * group_size + j
            columns.append(jnp.broadcast_to(left[:, at : at + 1], (rows, n)))
        scales = []
        for j in range(group_size):
            pivot = columns[j][j : j + 1, :]
            multiplier = jnp.where(row_index > j, columns[j] * (1.0 / pivot), 0.0)
            scales.append(lax.rsqrt(pivot))
            for k in range(j + 1, group_size):
                columns[k] = columns[k] - multiplier * columns[k][j : j + 1, :]
            if group < n // group_size - 1:
                left = left - multiplier * left[j : j + 1, :]
            right = right - multiplier * right[j : j + 1, :]
        finished.append(right[:group_size, :] * jnp.concatenate(scales, axis=0))
        left = left[group_size:, :]
        right = right[group_size:, :]
    return jnp.concatenate(finished, axis=0)


def eliminate_block(k, work, inverse):
    n = work.shape[0]
    low = k * block_size
    high = low + block_size
    diagonal = inverse_of_block_factor(work[low:high, low:high])
    inverse_rows = dot_exact(diagonal, inverse[low:high, :high], ((1,), (0,)))
    inverse[low:high, :high] = inverse_rows
    if high < n:
        factor_rows = dot_exact(diagonal, work[low:high, high:], ((1,), (0,)))
        work[high:, high:] = work[high:, high:] - dot_exact(factor_rows, factor_rows, ((0,), (0,)))
        inverse[high:, :high] = inverse[high:, :high] - dot_exact(
            factor_rows, inverse_rows, ((0,), (0,))
        )


def first_factor_kernel(own_ref, arrived_ref, work, inverse, token):
    token[...] = jnp.zeros_like(token)
    work[...] = own_ref[...] + arrived_ref[...]
    inverse[...] = identity(work.shape[0])
    eliminate_block(0, work, inverse)


def next_factor_kernel(k, work_in, inverse_in, token_in, work, inverse, token):
    token[...] = token_in[...]
    work[...] = work_in[...]
    inverse[...] = inverse_in[...]
    eliminate_block(k, work, inverse)


def factor_step(k, *operands):
    n = operands[0].shape[0]
    square = jax.ShapeDtypeStruct((n, n), f32)
    kernel = functools.partial(next_factor_kernel, k) if k else first_factor_kernel
    return pl.pallas_call(
        kernel,
        out_shape=(square, square, jax.ShapeDtypeStruct((8, tile), f32)),
        compiler_params=pltpu.CompilerParams(vmem_limit_bytes=12 * mebibyte),
        cost_estimate=pl.CostEstimate(flops=5 * 10**9, bytes_accessed=4 * n * n * 4, transcendentals=0),
    )(*operands)


def load_kernel(first, other_side, place_ref, parts_ref, rows_ref, semaphore):
    side = 1 - place_ref[1] if other_side else place_ref[1]
    copy = pltpu.make_async_copy(
        parts_ref.at[pl.ds(first, rows_ref.shape[0]), side], rows_ref, semaphore
    )
    copy.start()
    copy.wait()


def load_rows(blocks, place, first, other_side):
    _, _, rows, hidden = blocks.shape
    return pl.pallas_call(
        functools.partial(load_kernel, first, other_side),
        in_specs=[pl.BlockSpec(memory_space=pltpu.SMEM), pl.BlockSpec(memory_space=pltpu.HBM)],
        out_specs=pl.BlockSpec(memory_space=pltpu.VMEM),
        out_shape=jax.ShapeDtypeStruct((n_z // 2, rows, hidden), bf16),
        scratch_shapes=[pltpu.SemaphoreType.DMA],
        compiler_params=pltpu.CompilerParams(vmem_limit_bytes=8 * mebibyte),
        cost_estimate=pl.CostEstimate(flops=10**9, bytes_accessed=0, transcendentals=0),
    )(place, blocks)


def pair_kernel(place_ref, own_ref, other_ref, *refs):
    *out_refs, turned = refs
    n_blocks, rows, _ = own_ref.shape
    share = out_refs[0].shape[0]
    for block in range(n_blocks):
        total = own_ref[block].astype(f32) + other_ref[block].astype(f32)
        turned[...] = total.T.astype(bf16)
        for offset, out_ref in enumerate(out_refs):
            at = lax.rem(place_ref[0] + offset, n_z)
            chunk = turned[pl.ds(pl.multiple_of(at * share, share), share), :]
            out_ref[:, block * rows : (block + 1) * rows] = chunk


def pair_sum(place, own, other):
    n_blocks, rows, hidden = own.shape
    chunk = jax.ShapeDtypeStruct((hidden // n_z, n_blocks * rows), bf16)
    in_vmem = pl.BlockSpec(memory_space=pltpu.VMEM)
    return pl.pallas_call(
        pair_kernel,
        in_specs=[pl.BlockSpec(memory_space=pltpu.SMEM), in_vmem, in_vmem],
        out_specs=[in_vmem] * n_z,
        out_shape=[chunk] * n_z,
        scratch_shapes=[pltpu.VMEM((hidden, rows), bf16)],
        compiler_params=pltpu.CompilerParams(vmem_limit_bytes=12 * mebibyte),
        cost_estimate=pl.CostEstimate(flops=2 * 10**9, bytes_accessed=0, transcendentals=0),
    )(place, own, other)


def pick(blocks, index):
    return lax.dynamic_index_in_dim(blocks, index, 0, keepdims=False)


def swap(block):
    return lax.ppermute(block, "dp", swap_cores)


def together(*values):
    return lax.optimization_barrier(values)


def hop(up, down):
    up = lax.ppermute(up, "dp", z_shift(1))
    down = lax.ppermute(down, "dp", z_shift(-1))
    return up, down


def ring_term(own, moving):
    if moving is None:
        return own
    return (own.astype(f32) + moving.astype(f32)).astype(bf16)


def images_kernel(place_ref, *refs):
    *terms, basis_refs, gradient_ref, basis_ref, image_ref = (
        *refs[:6], refs[6 : 6 + n_z], *refs[6 + n_z :]
    )
    half = terms[0].shape[1]
    rows = basis_refs[0].shape[0]
    for side in range(2):
        own, up, down = (ref[...].astype(f32) for ref in terms[3 * side : 3 * side + 3])
        gradient_ref[:, side * half : (side + 1) * half] = (own + up + down).astype(bf16)
    for offset, ref in zip(ring_offsets, basis_refs):
        at = lax.rem(place_ref[0] + (n_z - offset), n_z)
        basis_ref[pl.ds(pl.multiple_of(at * rows, rows), rows), :] = ref[...]
    image_ref[...] = dot_fast(gradient_ref[...], basis_ref[...], ((1,), (0,)))


def sum_and_project(place, terms, basis_blocks):
    hidden, half = terms[0].shape
    rows, rank = basis_blocks[0].shape
    in_vmem = pl.BlockSpec(memory_space=pltpu.VMEM)
    return pl.pallas_call(
        images_kernel,
        in_specs=[pl.BlockSpec(memory_space=pltpu.SMEM)] + [in_vmem] * (len(terms) + n_z),
        out_shape=(
            jax.ShapeDtypeStruct((hidden, 2 * half), bf16),
            jax.ShapeDtypeStruct((n_z * rows, rank), bf16),
            jax.ShapeDtypeStruct((hidden, rank), f32),
        ),
        compiler_params=pltpu.CompilerParams(vmem_limit_bytes=16 * mebibyte),
    )(place, *terms, *basis_blocks)


def sum_gradient(local_parts, old_basis, place):
    d_model, hidden = local_parts.shape
    rows = d_model // (2 * n_z)
    blocks = local_parts.reshape(n_z, 2, rows, hidden)
    half = n_z // 2
    arrived = [swap(load_rows(blocks, place, first, True)) for first in (0, half)]
    kept_first, kept_second = [load_rows(blocks, place, first, False) for first in (0, half)]
    pieces = [list(pair_sum(place, *pair)) for pair in zip((kept_first, kept_second), arrived)]

    long_up = long_down = short_up = short_down = None
    old_basis, pieces[1][1] = together(old_basis, pieces[1][1])
    basis_up = basis_down = old_basis
    basis_blocks = [old_basis]
    for distance in range(half, 0, -1):
        long_up, long_down = hop(
            ring_term(pieces[0][distance], long_up),
            ring_term(pieces[1][-distance], long_down),
        )
        if distance > 2:
            basis_up, basis_down = hop(basis_up, basis_down)
            basis_blocks += [basis_up, basis_down]
        if distance > 1:
            short_up, short_down = hop(
                ring_term(pieces[1][distance - 1], short_up),
                ring_term(pieces[0][1 - distance], short_down),
            )
        if distance == 3:
            basis_up, basis_down = hop(basis_up, basis_down)
            basis_blocks += [basis_up, basis_down]
        if distance == 2:
            basis_blocks.append(lax.ppermute(basis_up, "dp", z_shift(1)))
        long_up, long_down = together(long_up, long_down)
        if distance > 1:
            short_up, short_down = together(short_up, short_down)
    terms = [pieces[0][0], long_up, short_down, pieces[1][0], short_up, long_down]
    return sum_and_project(place, terms, basis_blocks)


def back_kernel(gradient_ref, sketch_ref, back_ref):
    back_ref[...] = dot_fast(gradient_ref[...], sketch_ref[...], ((1,), (0,)))


def gram_kernel(sketch_ref, gram_ref):
    gram_ref[...] = dot_fast(sketch_ref[...], sketch_ref[...], ((0,), (0,)))


def small_call(kernel, rows, *operands):
    return pl.pallas_call(
        kernel,
        in_specs=[pl.BlockSpec(memory_space=pltpu.VMEM)] * len(operands),
        out_shape=jax.ShapeDtypeStruct((rows, operands[-1].shape[1]), f32),
        compiler_params=pltpu.CompilerParams(vmem_limit_bytes=16 * mebibyte),
        cost_estimate=pl.CostEstimate(flops=2 * 10**9, bytes_accessed=0, transcendentals=0),
    )(*operands)


def sum_blocks(blocks):
    return jnp.sum(blocks.astype(f32), axis=0).astype(bf16)


def spread_z(block):
    copies = jnp.broadcast_to(block[None], (n_z,) + block.shape)
    return lax.all_to_all(copies, "dp", 0, 0, tiled=True, axis_index_groups=z_groups)


def spread_rank(block):
    copies = jnp.broadcast_to(block[None], (lax.axis_size("rank"),) + block.shape)
    return lax.all_to_all(copies, "rank", 0, 0, tiled=True)


def split(values):
    high = values.astype(bf16)
    return high, (values - high.astype(f32)).astype(bf16)


def dot_split(left, right, dims):
    return dot_fast(left[0], right, dims) + dot_fast(left[1], right, dims)


def final_kernel(
    place_ref, inverse_ref, own_cosines_ref, other_cosines_ref, sketch_ref,
    own_moments_ref, other_moments_ref, own_back_ref, other_back_ref,
    basis_ref, moment_ref, second_ref, step_ref,
    first_in, second_in, back_in, update, moment_all, second_all,
):
    z, core = place_ref[0], place_ref[1]
    rank, hidden = first_in.shape
    share_rows = moment_ref.shape[0]
    hidden_own = hidden // (2 * n_z)
    for device_z in range(n_z):
        ring_z = lax.rem(z + (n_z - ring_offsets[device_z]), n_z)
        for side in range(2):
            mine = core == side
            device = ring_z * 2 + side
            rows = pl.ds(pl.multiple_of(device * share_rows, share_rows), share_rows)
            moments = jnp.where(mine, own_moments_ref[device_z], other_moments_ref[device_z])
            first_in[rows] = moments[:share_rows]
            second_in[rows] = moments[share_rows:]
            device = (z ^ flip_order[device_z]) * 2 + side
            rows = pl.ds(pl.multiple_of(device * hidden_own, 8), hidden_own)
            back_in[rows] = jnp.where(
                mine, own_back_ref[device_z].astype(f32), other_back_ref[device_z].astype(f32)
            )
    inverse = inverse_ref[...]
    inverse_split = split(inverse)
    sketch = sketch_ref[...]
    new_basis = (
        dot_fast(sketch, inverse_split[0], ((1,), (1,)))
        + dot_fast(sketch, inverse_split[1], ((1,), (1,)))
    ).astype(bf16)
    basis_ref[...] = new_basis
    cosines = split(own_cosines_ref[...] + other_cosines_ref[...])
    rotation = (
        dot_split(inverse_split, cosines[0], ((1,), (0,)))
        + dot_fast(inverse_split[0], cosines[1], ((1,), (0,)))
    )
    rotation_split = split(rotation)
    square_split = split(rotation * rotation)
    back_images = back_in[...].astype(bf16)
    step = 256
    for low in range(0, rank, step):
        rows = slice(low, low + step)
        projected = dot_split([v[rows] for v in inverse_split], back_images, ((1,), (1,)))
        first_rotated = dot_split([v[rows] for v in rotation_split], first_in[...], ((1,), (0,)))
        second_rotated = dot_split([v[rows] for v in square_split], second_in[...], ((1,), (0,)))
        moment_new = beta_one * first_rotated + (1.0 - beta_one) * projected
        second_new = beta_two * second_rotated + (1.0 - beta_two) * projected * projected
        moment_all[rows] = moment_new
        second_all[rows] = second_new
        update[rows] = (moment_new / (jnp.sqrt(second_new) + eps)).astype(bf16)
    own_rows = pl.ds(pl.multiple_of((z * 2 + core) * share_rows, share_rows), share_rows)
    moment_ref[...] = moment_all[own_rows]
    second_ref[...] = second_all[own_rows]
    step_ref[...] = dot_fast(new_basis, update[...], ((1,), (0,))).astype(bf16)


def final_step(place, inverse, cosines, sketch_own, moments, back_images):
    share_rows, hidden = moments[0].shape[1] // 2, moments[0].shape[2]
    rank = inverse.shape[0]
    rows = sketch_own.shape[0]
    in_vmem = pl.BlockSpec(memory_space=pltpu.VMEM)
    return pl.pallas_call(
        final_kernel,
        in_specs=[pl.BlockSpec(memory_space=pltpu.SMEM)] + [in_vmem] * 8,
        out_shape=(
            jax.ShapeDtypeStruct((rows, rank), bf16),
            jax.ShapeDtypeStruct((share_rows, hidden), f32),
            jax.ShapeDtypeStruct((share_rows, hidden), f32),
            jax.ShapeDtypeStruct((rows, hidden), bf16),
        ),
        scratch_shapes=[
            pltpu.VMEM((rank, hidden), bf16),
            pltpu.VMEM((rank, hidden), bf16),
            pltpu.VMEM((hidden, rank), f32),
            pltpu.VMEM((rank, hidden), bf16),
            pltpu.VMEM((rank, hidden), f32),
            pltpu.VMEM((rank, hidden), f32),
        ],
        compiler_params=pltpu.CompilerParams(vmem_limit_bytes=28 * mebibyte),
    )(place, inverse, *cosines, sketch_own, *moments, *back_images)


flip_order = (0, 4, 2, 6, 1, 5, 3, 7)

ring_offsets = (0, 1, 7, 2, 6, 3, 5, 4)


def on_device(grad_parts, old_basis, moment_one, moment_two):
    local_parts = grad_parts[0]
    d_model, hidden_share = local_parts.shape
    share_rows, rank = moment_one.shape[0], old_basis.shape[1]
    basis_rows = old_basis.shape[0]
    own = lax.axis_index("dp")
    z, core = lax.div(own, 2), lax.rem(own, 2)
    n_rank = lax.axis_size("rank")
    hidden_z = hidden_share // n_z
    moments = jnp.concatenate([moment_one, moment_two], axis=0).astype(bf16)

    place = jnp.stack([z, core]).astype(jnp.int32)
    gradient, basis_core, image_part = sum_gradient(local_parts, old_basis, place)
    images = split(image_part + swap(image_part))
    sketch_part = dot_fast(
        jnp.concatenate([gradient, gradient], axis=0), jnp.concatenate(images, axis=0), ((0,), (0,))
    ).astype(bf16)

    rows = d_model // 2 // n_rank
    sketch_part = sum_blocks(
        lax.all_to_all(sketch_part.reshape(n_rank, rows, rank), "rank", 0, 0, tiled=True)
    )
    sketch_rows = sum_blocks(
        lax.all_to_all(
            sketch_part.reshape(n_z, rows // n_z, rank), "dp", 0, 0, tiled=True, axis_index_groups=z_groups
        )
    )
    sketch_rows, moments = together(sketch_rows, moments)
    up = down = moments
    gathered = [moments]
    for distance in range(n_z // 2, 0, -1):
        if distance > 1:
            up, down = hop(up, down)
            up, down = together(up, down)
            gathered += [up, down]
        else:
            gathered.append(lax.ppermute(up, "dp", z_shift(1)))
    moments = jnp.stack(gathered)
    sketch = spread_z(sketch_rows).reshape(rows, rank)
    sketch = spread_rank(sketch).reshape(d_model // 2, rank)
    moments = (moments, swap(moments))

    back_part = small_call(back_kernel, hidden_z, gradient, sketch)
    back_part, sketch = together(back_part, sketch)
    back_part = back_part.reshape(2, hidden_z // 2, rank)
    back_other = swap(pick(back_part, 1 - core))
    gram_part = small_call(gram_kernel, rank, sketch)
    gram_other = swap(gram_part)
    cosine_part = dot_fast(sketch, basis_core, ((0,), (0,)))
    cosine_other = swap(cosine_part)

    back = (pick(back_part, core) + back_other).astype(bf16)[None]
    back, gram_other = together(back, gram_other)
    back = jnp.concatenate([back, lax.ppermute(back, "dp", z_flip(4))])
    *state, token = factor_step(0, gram_part, gram_other)
    for k, distance in ((1, 2), (2, 1)):
        back, token = together(back, token)
        back = jnp.concatenate([back, lax.ppermute(back, "dp", z_flip(distance))])
        *state, token = factor_step(k, *state, token)
    back, token = together(back, token)
    back = (back, swap(back))
    _, inverse, token = factor_step(3, *state, token)

    sketch_own = lax.dynamic_slice_in_dim(sketch, z * basis_rows, basis_rows, 0)
    return final_step(place, inverse, (cosine_part, cosine_other), sketch_own, moments, back)


def solution(mesh):
    in_specs = (P("dp", None, "rank"), P("dp", None), P("dp", "rank"), P("dp", "rank"))
    out_specs = (P("dp", None), P("dp", "rank"), P("dp", "rank"), P("dp", "rank"))
    return jax.shard_map(
        on_device, mesh=mesh, in_specs=in_specs, out_specs=out_specs, check_vma=False
    )
```

```python
import functools
import jax
import jax.numpy as jnp
from jax import lax
from jax.experimental import pallas as pl
from jax.experimental.pallas import tpu as pltpu
from jax.sharding import PartitionSpec as P

highest = lax.Precision.HIGHEST
beta_one = 0.9
beta_two = 0.95
eps = 1e-08
bf16 = jnp.bfloat16
f32 = jnp.float32
block_size = 128
group_size = 8

n_z = 8
swap_cores = [(z * 2 + c, z * 2 + 1 - c) for z in range(n_z) for c in range(2)]
z_groups = [[z * 2 + c for z in range(n_z)] for c in range(2)]
mebibyte = 1024 * 1024
tile = 128


def z_shift(step):
    return [(z * 2 + c, ((z + step) % n_z) * 2 + c) for z in range(n_z) for c in range(2)]


def z_flip(bit):
    return [(z * 2 + c, (z ^ bit) * 2 + c) for z in range(n_z) for c in range(2)]


def dot_exact(left, right, dims):
    return lax.dot_general(
        left, right, (dims, ((), ())), precision=highest, preferred_element_type=f32
    )


def dot_fast(left, right, dims):
    return lax.dot_general(left, right, (dims, ((), ())), preferred_element_type=f32)


def identity(n):
    return (
        lax.broadcasted_iota(jnp.int32, (n, n), 0) == lax.broadcasted_iota(jnp.int32, (n, n), 1)
    ).astype(f32)


def inverse_of_block_factor(block):
    n = block_size
    left = block
    right = identity(n)
    finished = []
    for group in range(n // group_size):
        rows = n - group * group_size
        row_index = lax.broadcasted_iota(jnp.int32, (rows, n), 0)
        columns = []
        for j in range(group_size):
            at = group * group_size + j
            columns.append(jnp.broadcast_to(left[:, at : at + 1], (rows, n)))
        scales = []
        for j in range(group_size):
            pivot = columns[j][j : j + 1, :]
            multiplier = jnp.where(row_index > j, columns[j] * (1.0 / pivot), 0.0)
            scales.append(lax.rsqrt(pivot))
            for k in range(j + 1, group_size):
                columns[k] = columns[k] - multiplier * columns[k][j : j + 1, :]
            if group < n // group_size - 1:
                left = left - multiplier * left[j : j + 1, :]
            right = right - multiplier * right[j : j + 1, :]
        finished.append(right[:group_size, :] * jnp.concatenate(scales, axis=0))
        left = left[group_size:, :]
        right = right[group_size:, :]
    return jnp.concatenate(finished, axis=0)


def eliminate_block(k, work, inverse):
    n = work.shape[0]
    low = k * block_size
    high = low + block_size
    diagonal = inverse_of_block_factor(work[low:high, low:high])
    inverse_rows = dot_exact(diagonal, inverse[low:high, :high], ((1,), (0,)))
    inverse[low:high, :high] = inverse_rows
    if high < n:
        factor_rows = dot_exact(diagonal, work[low:high, high:], ((1,), (0,)))
        work[high:, high:] = work[high:, high:] - dot_exact(factor_rows, factor_rows, ((0,), (0,)))
        inverse[high:, :high] = inverse[high:, :high] - dot_exact(
            factor_rows, inverse_rows, ((0,), (0,))
        )


def first_factor_kernel(own_ref, arrived_ref, work, inverse, token):
    token[...] = jnp.zeros_like(token)
    work[...] = own_ref[...] + arrived_ref[...]
    inverse[...] = identity(work.shape[0])
    eliminate_block(0, work, inverse)


def next_factor_kernel(k, work_in, inverse_in, token_in, work, inverse, token):
    token[...] = token_in[...]
    work[...] = work_in[...]
    inverse[...] = inverse_in[...]
    eliminate_block(k, work, inverse)


def factor_step(k, *operands):
    n = operands[0].shape[0]
    square = jax.ShapeDtypeStruct((n, n), f32)
    kernel = functools.partial(next_factor_kernel, k) if k else first_factor_kernel
    return pl.pallas_call(
        kernel,
        out_shape=(square, square, jax.ShapeDtypeStruct((8, tile), f32)),
        compiler_params=pltpu.CompilerParams(vmem_limit_bytes=12 * mebibyte),
        cost_estimate=pl.CostEstimate(flops=5 * 10**9, bytes_accessed=4 * n * n * 4, transcendentals=0),
    )(*operands)


def load_kernel(first, other_side, place_ref, parts_ref, rows_ref, semaphore):
    side = 1 - place_ref[1] if other_side else place_ref[1]
    copy = pltpu.make_async_copy(
        parts_ref.at[pl.ds(first, rows_ref.shape[0]), side], rows_ref, semaphore
    )
    copy.start()
    copy.wait()


def load_rows(blocks, place, first, other_side):
    _, _, rows, hidden = blocks.shape
    return pl.pallas_call(
        functools.partial(load_kernel, first, other_side),
        in_specs=[pl.BlockSpec(memory_space=pltpu.SMEM), pl.BlockSpec(memory_space=pltpu.HBM)],
        out_specs=pl.BlockSpec(memory_space=pltpu.VMEM),
        out_shape=jax.ShapeDtypeStruct((n_z // 2, rows, hidden), bf16),
        scratch_shapes=[pltpu.SemaphoreType.DMA],
        compiler_params=pltpu.CompilerParams(vmem_limit_bytes=8 * mebibyte),
        cost_estimate=pl.CostEstimate(flops=10**9, bytes_accessed=0, transcendentals=0),
    )(place, blocks)


def pair_kernel(place_ref, own_ref, other_ref, *refs):
    *out_refs, turned = refs
    n_blocks, rows, _ = own_ref.shape
    share = out_refs[0].shape[0]
    for block in range(n_blocks):
        total = own_ref[block].astype(f32) + other_ref[block].astype(f32)
        turned[...] = total.T.astype(bf16)
        for offset, out_ref in enumerate(out_refs):
            at = lax.rem(place_ref[0] + offset, n_z)
            chunk = turned[pl.ds(pl.multiple_of(at * share, share), share), :]
            out_ref[:, block * rows : (block + 1) * rows] = chunk


def pair_sum(place, own, other):
    n_blocks, rows, hidden = own.shape
    chunk = jax.ShapeDtypeStruct((hidden // n_z, n_blocks * rows), bf16)
    in_vmem = pl.BlockSpec(memory_space=pltpu.VMEM)
    return pl.pallas_call(
        pair_kernel,
        in_specs=[pl.BlockSpec(memory_space=pltpu.SMEM), in_vmem, in_vmem],
        out_specs=[in_vmem] * n_z,
        out_shape=[chunk] * n_z,
        scratch_shapes=[pltpu.VMEM((hidden, rows), bf16)],
        compiler_params=pltpu.CompilerParams(vmem_limit_bytes=12 * mebibyte),
        cost_estimate=pl.CostEstimate(flops=2 * 10**9, bytes_accessed=0, transcendentals=0),
    )(place, own, other)


def pick(blocks, index):
    return lax.dynamic_index_in_dim(blocks, index, 0, keepdims=False)


def swap(block):
    return lax.ppermute(block, "dp", swap_cores)


def together(*values):
    return lax.optimization_barrier(values)


def hop(up, down):
    up = lax.ppermute(up, "dp", z_shift(1))
    down = lax.ppermute(down, "dp", z_shift(-1))
    return up, down


def ring_term(own, moving):
    if moving is None:
        return own
    return (own.astype(f32) + moving.astype(f32)).astype(bf16)


def images_kernel(place_ref, *refs):
    terms, basis_refs, results = refs[:6], refs[6 : 7 + n_z], refs[7 + n_z :]
    gradient_ref, basis_ref, image_ref = results
    half = terms[0].shape[1]
    rows = basis_refs[0].shape[0]
    for side in range(2):
        own, up, down = (ref[...].astype(f32) for ref in terms[3 * side : 3 * side + 3])
        gradient_ref[:, side * half : (side + 1) * half] = (own + up + down).astype(bf16)
    for index, ref in enumerate(basis_refs):
        offset = ring_offsets[min(index, n_z - 1)]
        at = lax.rem(place_ref[0] + (n_z - offset), n_z) * rows
        if index == n_z:
            at = at + rows // 2
        basis_ref[pl.ds(pl.multiple_of(at, rows // 2), ref.shape[0]), :] = ref[...]
    image_ref[...] = dot_fast(gradient_ref[...], basis_ref[...], ((1,), (0,)))


def sum_and_project(place, terms, basis_blocks):
    hidden, half = terms[0].shape
    rows, rank = basis_blocks[0].shape
    in_vmem = pl.BlockSpec(memory_space=pltpu.VMEM)
    return pl.pallas_call(
        images_kernel,
        in_specs=[pl.BlockSpec(memory_space=pltpu.SMEM)] + [in_vmem] * (len(terms) + len(basis_blocks)),
        out_shape=(
            jax.ShapeDtypeStruct((hidden, 2 * half), bf16),
            jax.ShapeDtypeStruct((n_z * rows, rank), bf16),
            jax.ShapeDtypeStruct((hidden, rank), f32),
        ),
        compiler_params=pltpu.CompilerParams(vmem_limit_bytes=16 * mebibyte),
    )(place, *terms, *basis_blocks)


def sum_gradient(local_parts, old_basis, place):
    d_model, hidden = local_parts.shape
    rows = d_model // (2 * n_z)
    blocks = local_parts.reshape(n_z, 2, rows, hidden)
    half = n_z // 2
    arrived = [swap(load_rows(blocks, place, first, True)) for first in (0, half)]
    kept_first, kept_second = [load_rows(blocks, place, first, False) for first in (0, half)]
    basis_own, kept_first = together(old_basis, kept_first)
    basis_up, basis_down = hop(basis_own, basis_own)
    pieces = [list(pair_sum(place, *pair)) for pair in zip((kept_first, kept_second), arrived)]
    basis_up, basis_down, pieces[1][0] = together(basis_up, basis_down, pieces[1][0])
    basis_blocks = [old_basis, basis_up, basis_down]

    long_up = long_down = short_up = short_down = None
    for distance in range(half, 0, -1):
        if distance > 2:
            basis_up, basis_down = hop(basis_up, basis_down)
        elif distance == 2:
            part = old_basis.shape[0] // 2
            basis_up, basis_down = hop(basis_up[:part], basis_down[part:])
        long_up, long_down = hop(
            ring_term(pieces[0][distance], long_up),
            ring_term(pieces[1][-distance], long_down),
        )
        if distance > 1:
            short_up, short_down = hop(
                ring_term(pieces[1][distance - 1], short_up),
                ring_term(pieces[0][1 - distance], short_down),
            )
        if distance > 2:
            long_up, long_down, basis_up, basis_down = together(
                long_up, long_down, basis_up, basis_down
            )
            basis_blocks += [basis_up, basis_down]
        elif distance == 2:
            long_up, long_down = together(long_up, long_down)
            basis_blocks += [basis_up, basis_down]
        if distance > 1:
            short_up, short_down = together(short_up, short_down)
    terms = [pieces[0][0], long_up, short_down, pieces[1][0], short_up, long_down]
    return sum_and_project(place, terms, basis_blocks)


def back_kernel(gradient_ref, sketch_ref, back_ref):
    back_ref[...] = dot_fast(gradient_ref[...], sketch_ref[...], ((1,), (0,)))


def gram_kernel(sketch_ref, gram_ref):
    gram_ref[...] = dot_fast(sketch_ref[...], sketch_ref[...], ((0,), (0,)))


def small_call(kernel, rows, *operands):
    return pl.pallas_call(
        kernel,
        in_specs=[pl.BlockSpec(memory_space=pltpu.VMEM)] * len(operands),
        out_shape=jax.ShapeDtypeStruct((rows, operands[-1].shape[1]), f32),
        compiler_params=pltpu.CompilerParams(vmem_limit_bytes=16 * mebibyte),
        cost_estimate=pl.CostEstimate(flops=2 * 10**9, bytes_accessed=0, transcendentals=0),
    )(*operands)


def sum_blocks(blocks):
    return jnp.sum(blocks.astype(f32), axis=0).astype(bf16)


def spread_z(block):
    copies = jnp.broadcast_to(block[None], (n_z,) + block.shape)
    return lax.all_to_all(copies, "dp", 0, 0, tiled=True, axis_index_groups=z_groups)


def spread_rank(block):
    copies = jnp.broadcast_to(block[None], (lax.axis_size("rank"),) + block.shape)
    return lax.all_to_all(copies, "rank", 0, 0, tiled=True)


def split(values):
    high = values.astype(bf16)
    return high, (values - high.astype(f32)).astype(bf16)


def dot_split(left, right, dims):
    return dot_fast(left[0], right, dims) + dot_fast(left[1], right, dims)


def final_kernel(
    place_ref, inverse_ref, own_cosines_ref, other_cosines_ref, sketch_ref,
    own_moments_ref, other_moments_ref, own_back_ref, other_back_ref,
    basis_ref, moment_ref, second_ref, step_ref,
    first_in, second_in, back_in, update, moment_all, second_all,
):
    z, core = place_ref[0], place_ref[1]
    rank, hidden = first_in.shape
    share_rows = moment_ref.shape[0]
    hidden_own = hidden // (2 * n_z)
    for device_z in range(n_z):
        ring_z = lax.rem(z + (n_z - ring_offsets[device_z]), n_z)
        for side in range(2):
            mine = core == side
            device = ring_z * 2 + side
            rows = pl.ds(pl.multiple_of(device * share_rows, share_rows), share_rows)
            moments = jnp.where(mine, own_moments_ref[device_z], other_moments_ref[device_z])
            first_in[rows] = moments[:share_rows]
            second_in[rows] = moments[share_rows:]
            device = (z ^ flip_order[device_z]) * 2 + side
            rows = pl.ds(pl.multiple_of(device * hidden_own, 8), hidden_own)
            back_in[rows] = jnp.where(
                mine, own_back_ref[device_z].astype(f32), other_back_ref[device_z].astype(f32)
            )
    inverse = inverse_ref[...]
    inverse_split = split(inverse)
    sketch = sketch_ref[...]
    new_basis = (
        dot_fast(sketch, inverse_split[0], ((1,), (1,)))
        + dot_fast(sketch, inverse_split[1], ((1,), (1,)))
    ).astype(bf16)
    basis_ref[...] = new_basis
    cosines = split(own_cosines_ref[...] + other_cosines_ref[...])
    rotation = (
        dot_split(inverse_split, cosines[0], ((1,), (0,)))
        + dot_fast(inverse_split[0], cosines[1], ((1,), (0,)))
    )
    rotation_rounded = rotation.astype(bf16)
    square_rounded = (rotation * rotation).astype(bf16)
    back_images = back_in[...].astype(bf16)
    step = 256
    for low in range(0, rank, step):
        rows = slice(low, low + step)
        projected = dot_split([v[rows] for v in inverse_split], back_images, ((1,), (1,)))
        first_rotated = dot_fast(rotation_rounded[rows], first_in[...], ((1,), (0,)))
        second_rotated = dot_fast(square_rounded[rows], second_in[...], ((1,), (0,)))
        moment_new = beta_one * first_rotated + (1.0 - beta_one) * projected
        second_new = beta_two * second_rotated + (1.0 - beta_two) * projected * projected
        moment_all[rows] = moment_new
        second_all[rows] = second_new
        update[rows] = (moment_new / (jnp.sqrt(second_new) + eps)).astype(bf16)
    own_rows = pl.ds(pl.multiple_of((z * 2 + core) * share_rows, share_rows), share_rows)
    moment_ref[...] = moment_all[own_rows]
    second_ref[...] = second_all[own_rows]
    step_ref[...] = dot_fast(new_basis, update[...], ((1,), (0,))).astype(bf16)


def final_step(place, inverse, cosines, sketch_own, moments, back_images):
    share_rows, hidden = moments[0].shape[1] // 2, moments[0].shape[2]
    rank = inverse.shape[0]
    rows = sketch_own.shape[0]
    in_vmem = pl.BlockSpec(memory_space=pltpu.VMEM)
    return pl.pallas_call(
        final_kernel,
        in_specs=[pl.BlockSpec(memory_space=pltpu.SMEM)] + [in_vmem] * 8,
        out_shape=(
            jax.ShapeDtypeStruct((rows, rank), bf16),
            jax.ShapeDtypeStruct((share_rows, hidden), f32),
            jax.ShapeDtypeStruct((share_rows, hidden), f32),
            jax.ShapeDtypeStruct((rows, hidden), bf16),
        ),
        scratch_shapes=[
            pltpu.VMEM((rank, hidden), bf16),
            pltpu.VMEM((rank, hidden), bf16),
            pltpu.VMEM((hidden, rank), f32),
            pltpu.VMEM((rank, hidden), bf16),
            pltpu.VMEM((rank, hidden), f32),
            pltpu.VMEM((rank, hidden), f32),
        ],
        compiler_params=pltpu.CompilerParams(vmem_limit_bytes=28 * mebibyte),
    )(place, inverse, *cosines, sketch_own, *moments, *back_images)


flip_order = (0, 4, 2, 6, 1, 5, 3, 7)

ring_offsets = (0, 1, 7, 2, 6, 3, 5, 4)


def on_device(grad_parts, old_basis, moment_one, moment_two):
    local_parts = grad_parts[0]
    d_model, hidden_share = local_parts.shape
    share_rows, rank = moment_one.shape[0], old_basis.shape[1]
    basis_rows = old_basis.shape[0]
    own = lax.axis_index("dp")
    z, core = lax.div(own, 2), lax.rem(own, 2)
    n_rank = lax.axis_size("rank")
    hidden_z = hidden_share // n_z
    moments = jnp.concatenate([moment_one, moment_two], axis=0).astype(bf16)

    place = jnp.stack([z, core]).astype(jnp.int32)
    gradient, basis_core, image_part = sum_gradient(local_parts, old_basis, place)
    images = split(image_part + swap(image_part))
    sketch_part = dot_fast(
        jnp.concatenate([gradient, gradient], axis=0), jnp.concatenate(images, axis=0), ((0,), (0,))
    ).astype(bf16)

    rows = d_model // 2 // n_rank
    sketch_part = sum_blocks(
        lax.all_to_all(sketch_part.reshape(n_rank, rows, rank), "rank", 0, 0, tiled=True)
    )
    sketch_rows = sum_blocks(
        lax.all_to_all(
            sketch_part.reshape(n_z, rows // n_z, rank), "dp", 0, 0, tiled=True, axis_index_groups=z_groups
        )
    )
    sketch_rows, moments = together(sketch_rows, moments)
    up = down = moments
    gathered = [moments]
    for distance in range(n_z // 2, 0, -1):
        if distance > 1:
            up, down = hop(up, down)
            up, down = together(up, down)
            gathered += [up, down]
        else:
            gathered.append(lax.ppermute(up, "dp", z_shift(1)))
    moments = jnp.stack(gathered)
    sketch = spread_z(sketch_rows).reshape(rows, rank)
    sketch = spread_rank(sketch).reshape(d_model // 2, rank)
    moments = (moments, swap(moments))

    back_part = small_call(back_kernel, hidden_z, gradient, sketch)
    back_part, sketch = together(back_part, sketch)
    back_part = back_part.reshape(2, hidden_z // 2, rank)
    back_other = swap(pick(back_part, 1 - core))
    gram_part = small_call(gram_kernel, rank, sketch)
    gram_other = swap(gram_part)
    cosine_part = dot_fast(sketch, basis_core, ((0,), (0,)))
    cosine_other = swap(cosine_part)

    back = (pick(back_part, core) + back_other).astype(bf16)[None]
    back, gram_other = together(back, gram_other)
    back = jnp.concatenate([back, lax.ppermute(back, "dp", z_flip(4))])
    *state, token = factor_step(0, gram_part, gram_other)
    for k, distance in ((1, 2), (2, 1)):
        back, token = together(back, token)
        back = jnp.concatenate([back, lax.ppermute(back, "dp", z_flip(distance))])
        *state, token = factor_step(k, *state, token)
    back, token = together(back, token)
    back = (back, swap(back))
    _, inverse, token = factor_step(3, *state, token)

    sketch_own = lax.dynamic_slice_in_dim(sketch, z * basis_rows, basis_rows, 0)
    return final_step(place, inverse, (cosine_part, cosine_other), sketch_own, moments, back)


def solution(mesh):
    in_specs = (P("dp", None, "rank"), P("dp", None), P("dp", "rank"), P("dp", "rank"))
    out_specs = (P("dp", None), P("dp", "rank"), P("dp", "rank"), P("dp", "rank"))
    return jax.shard_map(
        on_device, mesh=mesh, in_specs=in_specs, out_specs=out_specs, check_vma=False
    )
```

```python
import functools
import jax
import jax.numpy as jnp
from jax import lax
from jax.experimental import pallas as pl
from jax.experimental.pallas import tpu as pltpu
from jax.sharding import PartitionSpec as P

highest = lax.Precision.HIGHEST
beta_one = 0.9
beta_two = 0.95
eps = 1e-08
bf16 = jnp.bfloat16
f32 = jnp.float32
block_size = 128
group_size = 8

n_z = 8
swap_cores = [(z * 2 + c, z * 2 + 1 - c) for z in range(n_z) for c in range(2)]
z_groups = [[z * 2 + c for z in range(n_z)] for c in range(2)]
mebibyte = 1024 * 1024
tile = 128


def z_shift(step):
    return [(z * 2 + c, ((z + step) % n_z) * 2 + c) for z in range(n_z) for c in range(2)]


def z_flip(bit):
    return [(z * 2 + c, (z ^ bit) * 2 + c) for z in range(n_z) for c in range(2)]


def dot_exact(left, right, dims):
    return lax.dot_general(
        left, right, (dims, ((), ())), precision=highest, preferred_element_type=f32
    )


def dot_fast(left, right, dims):
    return lax.dot_general(left, right, (dims, ((), ())), preferred_element_type=f32)


def identity(n):
    return (
        lax.broadcasted_iota(jnp.int32, (n, n), 0) == lax.broadcasted_iota(jnp.int32, (n, n), 1)
    ).astype(f32)


def inverse_of_block_factor(block):
    n = block_size
    left = block
    right = identity(n)
    finished = []
    for group in range(n // group_size):
        rows = n - group * group_size
        row_index = lax.broadcasted_iota(jnp.int32, (rows, n), 0)
        columns = []
        for j in range(group_size):
            at = group * group_size + j
            columns.append(jnp.broadcast_to(left[:, at : at + 1], (rows, n)))
        scales = []
        for j in range(group_size):
            pivot = columns[j][j : j + 1, :]
            multiplier = jnp.where(row_index > j, columns[j] * (1.0 / pivot), 0.0)
            scales.append(lax.rsqrt(pivot))
            for k in range(j + 1, group_size):
                columns[k] = columns[k] - multiplier * columns[k][j : j + 1, :]
            if group < n // group_size - 1:
                left = left - multiplier * left[j : j + 1, :]
            right = right - multiplier * right[j : j + 1, :]
        finished.append(right[:group_size, :] * jnp.concatenate(scales, axis=0))
        left = left[group_size:, :]
        right = right[group_size:, :]
    return jnp.concatenate(finished, axis=0)


def eliminate_block(k, work, inverse):
    n = work.shape[0]
    low = k * block_size
    high = low + block_size
    diagonal = inverse_of_block_factor(work[low:high, low:high])
    inverse_rows = dot_exact(diagonal, inverse[low:high, :high], ((1,), (0,)))
    inverse[low:high, :high] = inverse_rows
    if high < n:
        factor_rows = dot_exact(diagonal, work[low:high, high:], ((1,), (0,)))
        work[high:, high:] = work[high:, high:] - dot_exact(factor_rows, factor_rows, ((0,), (0,)))
        inverse[high:, :high] = inverse[high:, :high] - dot_exact(
            factor_rows, inverse_rows, ((0,), (0,))
        )


def first_factor_kernel(own_ref, arrived_ref, work, inverse, token):
    token[...] = jnp.zeros_like(token)
    work[...] = own_ref[...] + arrived_ref[...]
    inverse[...] = identity(work.shape[0])
    eliminate_block(0, work, inverse)


def next_factor_kernel(k, work_in, inverse_in, token_in, work, inverse, token):
    token[...] = token_in[...]
    low = k * block_size
    n = work.shape[0]
    work[low:, low:] = work_in[low:, low:]
    inverse[:, :low] = inverse_in[:, :low]
    inverse[:low, low:] = jnp.zeros((low, n - low), f32)
    inverse[low:, low:] = identity(n - low)
    eliminate_block(k, work, inverse)


def factor_step(k, *operands):
    n = operands[0].shape[0]
    square = jax.ShapeDtypeStruct((n, n), f32)
    kernel = functools.partial(next_factor_kernel, k) if k else first_factor_kernel
    return pl.pallas_call(
        kernel,
        out_shape=(square, square, jax.ShapeDtypeStruct((8, tile), f32)),
        compiler_params=pltpu.CompilerParams(vmem_limit_bytes=12 * mebibyte),
        cost_estimate=pl.CostEstimate(flops=5 * 10**9, bytes_accessed=4 * n * n * 4, transcendentals=0),
    )(*operands)


def load_kernel(first, other_side, place_ref, parts_ref, rows_ref, semaphore):
    side = 1 - place_ref[1] if other_side else place_ref[1]
    copy = pltpu.make_async_copy(
        parts_ref.at[pl.ds(first, rows_ref.shape[0]), side], rows_ref, semaphore
    )
    copy.start()
    copy.wait()


def load_rows(blocks, place, first, other_side):
    _, _, rows, hidden = blocks.shape
    return pl.pallas_call(
        functools.partial(load_kernel, first, other_side),
        in_specs=[pl.BlockSpec(memory_space=pltpu.SMEM), pl.BlockSpec(memory_space=pltpu.HBM)],
        out_specs=pl.BlockSpec(memory_space=pltpu.VMEM),
        out_shape=jax.ShapeDtypeStruct((n_z // 2, rows, hidden), bf16),
        scratch_shapes=[pltpu.SemaphoreType.DMA],
        compiler_params=pltpu.CompilerParams(vmem_limit_bytes=8 * mebibyte),
        cost_estimate=pl.CostEstimate(flops=10**9, bytes_accessed=0, transcendentals=0),
    )(place, blocks)


def pair_kernel(place_ref, own_ref, other_ref, *refs):
    *out_refs, turned = refs
    n_blocks, rows, _ = own_ref.shape
    share = out_refs[0].shape[0]
    for block in range(n_blocks):
        total = own_ref[block].astype(f32) + other_ref[block].astype(f32)
        turned[...] = total.T.astype(bf16)
        for offset, out_ref in enumerate(out_refs):
            at = lax.rem(place_ref[0] + offset, n_z)
            chunk = turned[pl.ds(pl.multiple_of(at * share, share), share), :]
            out_ref[:, block * rows : (block + 1) * rows] = chunk


def pair_sum(place, own, other):
    n_blocks, rows, hidden = own.shape
    chunk = jax.ShapeDtypeStruct((hidden // n_z, n_blocks * rows), bf16)
    in_vmem = pl.BlockSpec(memory_space=pltpu.VMEM)
    return pl.pallas_call(
        pair_kernel,
        in_specs=[pl.BlockSpec(memory_space=pltpu.SMEM), in_vmem, in_vmem],
        out_specs=[in_vmem] * n_z,
        out_shape=[chunk] * n_z,
        scratch_shapes=[pltpu.VMEM((hidden, rows), bf16)],
        compiler_params=pltpu.CompilerParams(vmem_limit_bytes=12 * mebibyte),
        cost_estimate=pl.CostEstimate(flops=2 * 10**9, bytes_accessed=0, transcendentals=0),
    )(place, own, other)


def pick(blocks, index):
    return lax.dynamic_index_in_dim(blocks, index, 0, keepdims=False)


def swap(block):
    return lax.ppermute(block, "dp", swap_cores)


def together(*values):
    return lax.optimization_barrier(values)


def hop(up, down):
    up = lax.ppermute(up, "dp", z_shift(1))
    down = lax.ppermute(down, "dp", z_shift(-1))
    return up, down


def ring_term(own, moving):
    if moving is None:
        return own
    return (own.astype(f32) + moving.astype(f32)).astype(bf16)


def images_kernel(place_ref, *refs):
    terms, basis_refs, results = refs[:6], refs[6 : 7 + n_z], refs[7 + n_z :]
    gradient_ref, basis_ref, image_ref = results
    half = terms[0].shape[1]
    rows = basis_refs[0].shape[0]
    for side in range(2):
        own, up, down = (ref[...].astype(f32) for ref in terms[3 * side : 3 * side + 3])
        gradient_ref[:, side * half : (side + 1) * half] = (own + up + down).astype(bf16)
    for index, ref in enumerate(basis_refs):
        offset = ring_offsets[min(index, n_z - 1)]
        at = lax.rem(place_ref[0] + (n_z - offset), n_z) * rows
        if index == n_z:
            at = at + rows // 2
        basis_ref[pl.ds(pl.multiple_of(at, rows // 2), ref.shape[0]), :] = ref[...]
    image_ref[...] = dot_fast(gradient_ref[...], basis_ref[...], ((1,), (0,)))


def sum_and_project(place, terms, basis_blocks):
    hidden, half = terms[0].shape
    rows, rank = basis_blocks[0].shape
    in_vmem = pl.BlockSpec(memory_space=pltpu.VMEM)
    return pl.pallas_call(
        images_kernel,
        in_specs=[pl.BlockSpec(memory_space=pltpu.SMEM)] + [in_vmem] * (len(terms) + len(basis_blocks)),
        out_shape=(
            jax.ShapeDtypeStruct((hidden, 2 * half), bf16),
            jax.ShapeDtypeStruct((n_z * rows, rank), bf16),
            jax.ShapeDtypeStruct((hidden, rank), f32),
        ),
        compiler_params=pltpu.CompilerParams(vmem_limit_bytes=16 * mebibyte),
    )(place, *terms, *basis_blocks)


def sum_gradient(local_parts, old_basis, place):
    d_model, hidden = local_parts.shape
    rows = d_model // (2 * n_z)
    blocks = local_parts.reshape(n_z, 2, rows, hidden)
    half = n_z // 2
    arrived = [swap(load_rows(blocks, place, first, True)) for first in (0, half)]
    kept_first, kept_second = [load_rows(blocks, place, first, False) for first in (0, half)]
    basis_own, kept_first = together(old_basis, kept_first)
    basis_up, basis_down = hop(basis_own, basis_own)
    pieces = [list(pair_sum(place, *pair)) for pair in zip((kept_first, kept_second), arrived)]
    basis_up, basis_down, pieces[1][0] = together(basis_up, basis_down, pieces[1][0])
    basis_blocks = [old_basis, basis_up, basis_down]

    long_up = long_down = short_up = short_down = None
    for distance in range(half, 0, -1):
        if distance > 2:
            basis_up, basis_down = hop(basis_up, basis_down)
        elif distance == 2:
            part = old_basis.shape[0] // 2
            basis_up, basis_down = hop(basis_up[:part], basis_down[part:])
        long_up, long_down = hop(
            ring_term(pieces[0][distance], long_up),
            ring_term(pieces[1][-distance], long_down),
        )
        if distance > 1:
            short_up, short_down = hop(
                ring_term(pieces[1][distance - 1], short_up),
                ring_term(pieces[0][1 - distance], short_down),
            )
        if distance > 2:
            long_up, long_down, basis_up, basis_down = together(
                long_up, long_down, basis_up, basis_down
            )
            basis_blocks += [basis_up, basis_down]
        elif distance == 2:
            long_up, long_down = together(long_up, long_down)
            basis_blocks += [basis_up, basis_down]
        if distance > 1:
            short_up, short_down = together(short_up, short_down)
    terms = [pieces[0][0], long_up, short_down, pieces[1][0], short_up, long_down]
    return sum_and_project(place, terms, basis_blocks)


def back_kernel(gradient_ref, sketch_ref, back_ref):
    back_ref[...] = dot_fast(gradient_ref[...], sketch_ref[...], ((1,), (0,)))


def gram_kernel(sketch_ref, gram_ref):
    gram_ref[...] = dot_fast(sketch_ref[...], sketch_ref[...], ((0,), (0,)))


def small_call(kernel, rows, *operands):
    return pl.pallas_call(
        kernel,
        in_specs=[pl.BlockSpec(memory_space=pltpu.VMEM)] * len(operands),
        out_shape=jax.ShapeDtypeStruct((rows, operands[-1].shape[1]), f32),
        compiler_params=pltpu.CompilerParams(vmem_limit_bytes=16 * mebibyte),
        cost_estimate=pl.CostEstimate(flops=2 * 10**9, bytes_accessed=0, transcendentals=0),
    )(*operands)


def sum_blocks(blocks):
    return jnp.sum(blocks.astype(f32), axis=0).astype(bf16)


def spread_z(block):
    copies = jnp.broadcast_to(block[None], (n_z,) + block.shape)
    return lax.all_to_all(copies, "dp", 0, 0, tiled=True, axis_index_groups=z_groups)


def spread_rank(block):
    copies = jnp.broadcast_to(block[None], (lax.axis_size("rank"),) + block.shape)
    return lax.all_to_all(copies, "rank", 0, 0, tiled=True)


def split(values):
    high = values.astype(bf16)
    return high, (values - high.astype(f32)).astype(bf16)


def dot_split(left, right, dims):
    return dot_fast(left[0], right, dims) + dot_fast(left[1], right, dims)


def final_kernel(
    place_ref, inverse_ref, own_cosines_ref, other_cosines_ref, sketch_ref,
    own_moments_ref, other_moments_ref, own_back_ref, other_back_ref,
    basis_ref, moment_ref, second_ref, step_ref,
    first_in, second_in, back_in, update, moment_all, second_all,
):
    z, core = place_ref[0], place_ref[1]
    rank, hidden = first_in.shape
    share_rows = moment_ref.shape[0]
    hidden_own = hidden // (2 * n_z)
    for device_z in range(n_z):
        ring_z = lax.rem(z + (n_z - ring_offsets[device_z]), n_z)
        for side in range(2):
            mine = core == side
            device = ring_z * 2 + side
            rows = pl.ds(pl.multiple_of(device * share_rows, share_rows), share_rows)
            moments = jnp.where(mine, own_moments_ref[device_z], other_moments_ref[device_z])
            first_in[rows] = moments[:share_rows]
            second_in[rows] = moments[share_rows:]
            device = (z ^ flip_order[device_z]) * 2 + side
            rows = pl.ds(pl.multiple_of(device * hidden_own, 8), hidden_own)
            back_in[rows] = jnp.where(
                mine, own_back_ref[device_z].astype(f32), other_back_ref[device_z].astype(f32)
            )
    inverse = inverse_ref[...]
    inverse_split = split(inverse)
    sketch = sketch_ref[...]
    new_basis = (
        dot_fast(sketch, inverse_split[0], ((1,), (1,)))
        + dot_fast(sketch, inverse_split[1], ((1,), (1,)))
    ).astype(bf16)
    basis_ref[...] = new_basis
    cosines = split(own_cosines_ref[...] + other_cosines_ref[...])
    rotation = (
        dot_split(inverse_split, cosines[0], ((1,), (0,)))
        + dot_fast(inverse_split[0], cosines[1], ((1,), (0,)))
    )
    rotation_rounded = rotation.astype(bf16)
    square_rounded = (rotation * rotation).astype(bf16)
    back_images = back_in[...].astype(bf16)
    step = 256
    for low in range(0, rank, step):
        rows = slice(low, low + step)
        projected = dot_split([v[rows] for v in inverse_split], back_images, ((1,), (1,)))
        first_rotated = dot_fast(rotation_rounded[rows], first_in[...], ((1,), (0,)))
        second_rotated = dot_fast(square_rounded[rows], second_in[...], ((1,), (0,)))
        moment_new = beta_one * first_rotated + (1.0 - beta_one) * projected
        second_new = beta_two * second_rotated + (1.0 - beta_two) * projected * projected
        moment_all[rows] = moment_new
        second_all[rows] = second_new
        update[rows] = (moment_new / (jnp.sqrt(second_new) + eps)).astype(bf16)
    own_rows = pl.ds(pl.multiple_of((z * 2 + core) * share_rows, share_rows), share_rows)
    moment_ref[...] = moment_all[own_rows]
    second_ref[...] = second_all[own_rows]
    step_ref[...] = dot_fast(new_basis, update[...], ((1,), (0,))).astype(bf16)


def final_step(place, inverse, cosines, sketch_own, moments, back_images):
    share_rows, hidden = moments[0].shape[1] // 2, moments[0].shape[2]
    rank = inverse.shape[0]
    rows = sketch_own.shape[0]
    in_vmem = pl.BlockSpec(memory_space=pltpu.VMEM)
    return pl.pallas_call(
        final_kernel,
        in_specs=[pl.BlockSpec(memory_space=pltpu.SMEM)] + [in_vmem] * 8,
        out_shape=(
            jax.ShapeDtypeStruct((rows, rank), bf16),
            jax.ShapeDtypeStruct((share_rows, hidden), f32),
            jax.ShapeDtypeStruct((share_rows, hidden), f32),
            jax.ShapeDtypeStruct((rows, hidden), bf16),
        ),
        scratch_shapes=[
            pltpu.VMEM((rank, hidden), bf16),
            pltpu.VMEM((rank, hidden), bf16),
            pltpu.VMEM((hidden, rank), f32),
            pltpu.VMEM((rank, hidden), bf16),
            pltpu.VMEM((rank, hidden), f32),
            pltpu.VMEM((rank, hidden), f32),
        ],
        compiler_params=pltpu.CompilerParams(vmem_limit_bytes=28 * mebibyte),
    )(place, inverse, *cosines, sketch_own, *moments, *back_images)


flip_order = (0, 4, 2, 6, 1, 5, 3, 7)

ring_offsets = (0, 1, 7, 2, 6, 3, 5, 4)


def on_device(grad_parts, old_basis, moment_one, moment_two):
    local_parts = grad_parts[0]
    d_model, hidden_share = local_parts.shape
    share_rows, rank = moment_one.shape[0], old_basis.shape[1]
    basis_rows = old_basis.shape[0]
    own = lax.axis_index("dp")
    z, core = lax.div(own, 2), lax.rem(own, 2)
    n_rank = lax.axis_size("rank")
    hidden_z = hidden_share // n_z
    moments = jnp.concatenate([moment_one, moment_two], axis=0).astype(bf16)

    place = jnp.stack([z, core]).astype(jnp.int32)
    gradient, basis_core, image_part = sum_gradient(local_parts, old_basis, place)
    images = split(image_part + swap(image_part))
    sketch_part = dot_fast(
        jnp.concatenate([gradient, gradient], axis=0), jnp.concatenate(images, axis=0), ((0,), (0,))
    ).astype(bf16)

    rows = d_model // 2 // n_rank
    sketch_part = sum_blocks(
        lax.all_to_all(sketch_part.reshape(n_rank, rows, rank), "rank", 0, 0, tiled=True)
    )
    sketch_rows = sum_blocks(
        lax.all_to_all(
            sketch_part.reshape(n_z, rows // n_z, rank), "dp", 0, 0, tiled=True, axis_index_groups=z_groups
        )
    )
    sketch_rows, moments = together(sketch_rows, moments)
    up = down = moments
    gathered = [moments]
    for distance in range(n_z // 2, 0, -1):
        if distance > 1:
            up, down = hop(up, down)
            up, down = together(up, down)
            gathered += [up, down]
        else:
            gathered.append(lax.ppermute(up, "dp", z_shift(1)))
    moments = jnp.stack(gathered)
    sketch = spread_z(sketch_rows).reshape(rows, rank)
    sketch = spread_rank(sketch).reshape(d_model // 2, rank)
    moments = (moments, swap(moments))

    back_part = small_call(back_kernel, hidden_z, gradient, sketch)
    back_part, sketch = together(back_part, sketch)
    back_part = back_part.reshape(2, hidden_z // 2, rank)
    back_other = swap(pick(back_part, 1 - core))
    gram_part = small_call(gram_kernel, rank, sketch)
    gram_other = swap(gram_part)
    cosine_part = dot_fast(sketch, basis_core, ((0,), (0,)))
    cosine_other = swap(cosine_part)

    back = (pick(back_part, core) + back_other).astype(bf16)[None]
    back, gram_other = together(back, gram_other)
    back = jnp.concatenate([back, lax.ppermute(back, "dp", z_flip(4))])
    *state, token = factor_step(0, gram_part, gram_other)
    for k, distance in ((1, 2), (2, 1)):
        back, token = together(back, token)
        back = jnp.concatenate([back, lax.ppermute(back, "dp", z_flip(distance))])
        *state, token = factor_step(k, *state, token)
    back, token = together(back, token)
    back = (back, swap(back))
    _, inverse, token = factor_step(3, *state, token)

    sketch_own = lax.dynamic_slice_in_dim(sketch, z * basis_rows, basis_rows, 0)
    return final_step(place, inverse, (cosine_part, cosine_other), sketch_own, moments, back)


def solution(mesh):
    in_specs = (P("dp", None, "rank"), P("dp", None), P("dp", "rank"), P("dp", "rank"))
    out_specs = (P("dp", None), P("dp", "rank"), P("dp", "rank"), P("dp", "rank"))
    return jax.shard_map(
        on_device, mesh=mesh, in_specs=in_specs, out_specs=out_specs, check_vma=False
    )
```

```python
import functools
import jax
import jax.numpy as jnp
from jax import lax
from jax.experimental import pallas as pl
from jax.experimental.pallas import tpu as pltpu
from jax.sharding import PartitionSpec as P

highest = lax.Precision.HIGHEST
beta_one = 0.9
beta_two = 0.95
eps = 1e-08
bf16 = jnp.bfloat16
f32 = jnp.float32
block_size = 128
group_size = 8

n_z = 8
swap_cores = [(z * 2 + c, z * 2 + 1 - c) for z in range(n_z) for c in range(2)]
z_groups = [[z * 2 + c for z in range(n_z)] for c in range(2)]
mebibyte = 1024 * 1024
tile = 128


def z_shift(step):
    return [(z * 2 + c, ((z + step) % n_z) * 2 + c) for z in range(n_z) for c in range(2)]


def z_flip(bit):
    return [(z * 2 + c, (z ^ bit) * 2 + c) for z in range(n_z) for c in range(2)]


def dot_exact(left, right, dims):
    return lax.dot_general(
        left, right, (dims, ((), ())), precision=highest, preferred_element_type=f32
    )


def dot_fast(left, right, dims):
    return lax.dot_general(left, right, (dims, ((), ())), preferred_element_type=f32)


def identity(n):
    return (
        lax.broadcasted_iota(jnp.int32, (n, n), 0) == lax.broadcasted_iota(jnp.int32, (n, n), 1)
    ).astype(f32)


def inverse_of_block_factor(block):
    n = block_size
    left = block
    right = identity(n)
    finished = []
    for group in range(n // group_size):
        rows = n - group * group_size
        row_index = lax.broadcasted_iota(jnp.int32, (rows, n), 0)
        columns = []
        for j in range(group_size):
            at = group * group_size + j
            columns.append(jnp.broadcast_to(left[:, at : at + 1], (rows, n)))
        scales = []
        for j in range(group_size):
            pivot = columns[j][j : j + 1, :]
            multiplier = jnp.where(row_index > j, columns[j] * (1.0 / pivot), 0.0)
            scales.append(lax.rsqrt(pivot))
            for k in range(j + 1, group_size):
                columns[k] = columns[k] - multiplier * columns[k][j : j + 1, :]
            if group < n // group_size - 1:
                left = left - multiplier * left[j : j + 1, :]
            right = right - multiplier * right[j : j + 1, :]
        finished.append(right[:group_size, :] * jnp.concatenate(scales, axis=0))
        left = left[group_size:, :]
        right = right[group_size:, :]
    return jnp.concatenate(finished, axis=0)


def eliminate_block(k, work, inverse):
    n = work.shape[0]
    low = k * block_size
    high = low + block_size
    diagonal = inverse_of_block_factor(work[low:high, low:high])
    inverse_rows = dot_exact(diagonal, inverse[low:high, :high], ((1,), (0,)))
    inverse[low:high, :high] = inverse_rows
    if high < n:
        factor_rows = dot_exact(diagonal, work[low:high, high:], ((1,), (0,)))
        work[high:, high:] = work[high:, high:] - dot_exact(factor_rows, factor_rows, ((0,), (0,)))
        inverse[high:, :high] = inverse[high:, :high] - dot_exact(
            factor_rows, inverse_rows, ((0,), (0,))
        )


def first_factor_kernel(own_ref, arrived_ref, work, inverse, token):
    token[...] = jnp.zeros_like(token)
    work[...] = own_ref[...] + arrived_ref[...]
    inverse[...] = identity(work.shape[0])
    eliminate_block(0, work, inverse)


def next_factor_kernel(k, work_in, inverse_in, token_in, work, inverse, token):
    token[...] = token_in[...]
    low = k * block_size
    n = work.shape[0]
    work[low:, low:] = work_in[low:, low:]
    inverse[:, :low] = inverse_in[:, :low]
    inverse[:low, low:] = jnp.zeros((low, n - low), f32)
    inverse[low:, low:] = identity(n - low)
    eliminate_block(k, work, inverse)


def factor_step(k, *operands):
    n = operands[0].shape[0]
    square = jax.ShapeDtypeStruct((n, n), f32)
    kernel = functools.partial(next_factor_kernel, k) if k else first_factor_kernel
    return pl.pallas_call(
        kernel,
        out_shape=(square, square, jax.ShapeDtypeStruct((8, tile), f32)),
        compiler_params=pltpu.CompilerParams(vmem_limit_bytes=12 * mebibyte),
        cost_estimate=pl.CostEstimate(flops=5 * 10**9, bytes_accessed=4 * n * n * 4, transcendentals=0),
    )(*operands)


def load_kernel(first, other_side, place_ref, parts_ref, rows_ref, semaphore):
    side = 1 - place_ref[1] if other_side else place_ref[1]
    copy = pltpu.make_async_copy(
        parts_ref.at[pl.ds(first, rows_ref.shape[0]), side], rows_ref, semaphore
    )
    copy.start()
    copy.wait()


def load_rows(blocks, place, first, other_side):
    _, _, rows, hidden = blocks.shape
    return pl.pallas_call(
        functools.partial(load_kernel, first, other_side),
        in_specs=[pl.BlockSpec(memory_space=pltpu.SMEM), pl.BlockSpec(memory_space=pltpu.HBM)],
        out_specs=pl.BlockSpec(memory_space=pltpu.VMEM),
        out_shape=jax.ShapeDtypeStruct((n_z // 2, rows, hidden), bf16),
        scratch_shapes=[pltpu.SemaphoreType.DMA],
        compiler_params=pltpu.CompilerParams(vmem_limit_bytes=8 * mebibyte),
        cost_estimate=pl.CostEstimate(flops=10**9, bytes_accessed=0, transcendentals=0),
    )(place, blocks)


def pair_kernel(place_ref, own_ref, other_ref, *refs):
    *out_refs, turned = refs
    n_blocks, rows, _ = own_ref.shape
    share = out_refs[0].shape[0]
    for block in range(n_blocks):
        total = own_ref[block].astype(f32) + other_ref[block].astype(f32)
        turned[...] = total.T.astype(bf16)
        for offset, out_ref in enumerate(out_refs):
            at = lax.rem(place_ref[0] + offset, n_z)
            chunk = turned[pl.ds(pl.multiple_of(at * share, share), share), :]
            out_ref[:, block * rows : (block + 1) * rows] = chunk


def pair_sum(place, own, other):
    n_blocks, rows, hidden = own.shape
    chunk = jax.ShapeDtypeStruct((hidden // n_z, n_blocks * rows), bf16)
    in_vmem = pl.BlockSpec(memory_space=pltpu.VMEM)
    return pl.pallas_call(
        pair_kernel,
        in_specs=[pl.BlockSpec(memory_space=pltpu.SMEM), in_vmem, in_vmem],
        out_specs=[in_vmem] * n_z,
        out_shape=[chunk] * n_z,
        scratch_shapes=[pltpu.VMEM((hidden, rows), bf16)],
        compiler_params=pltpu.CompilerParams(vmem_limit_bytes=12 * mebibyte),
        cost_estimate=pl.CostEstimate(flops=2 * 10**9, bytes_accessed=0, transcendentals=0),
    )(place, own, other)


def pick(blocks, index):
    return lax.dynamic_index_in_dim(blocks, index, 0, keepdims=False)


def swap(block):
    return lax.ppermute(block, "dp", swap_cores)


def together(*values):
    return lax.optimization_barrier(values)


def hop(up, down):
    up = lax.ppermute(up, "dp", z_shift(1))
    down = lax.ppermute(down, "dp", z_shift(-1))
    return up, down


def ring_term(own, moving):
    if moving is None:
        return own
    return (own.astype(f32) + moving.astype(f32)).astype(bf16)


def images_kernel(place_ref, *refs):
    terms, basis_refs, results = refs[:6], refs[6 : 7 + n_z], refs[7 + n_z :]
    gradient_ref, basis_ref, image_ref = results
    half = terms[0].shape[1]
    rows = basis_refs[0].shape[0]
    for side in range(2):
        own, up, down = (ref[...].astype(f32) for ref in terms[3 * side : 3 * side + 3])
        gradient_ref[:, side * half : (side + 1) * half] = (own + up + down).astype(bf16)
    for index, ref in enumerate(basis_refs):
        offset = ring_offsets[min(index, n_z - 1)]
        at = lax.rem(place_ref[0] + (n_z - offset), n_z) * rows
        if index == n_z:
            at = at + rows // 2
        basis_ref[pl.ds(pl.multiple_of(at, rows // 2), ref.shape[0]), :] = ref[...]
    image_ref[...] = dot_fast(gradient_ref[...], basis_ref[...], ((1,), (0,)))


def sum_and_project(place, terms, basis_blocks):
    hidden, half = terms[0].shape
    rows, rank = basis_blocks[0].shape
    in_vmem = pl.BlockSpec(memory_space=pltpu.VMEM)
    return pl.pallas_call(
        images_kernel,
        in_specs=[pl.BlockSpec(memory_space=pltpu.SMEM)] + [in_vmem] * (len(terms) + len(basis_blocks)),
        out_shape=(
            jax.ShapeDtypeStruct((hidden, 2 * half), bf16),
            jax.ShapeDtypeStruct((n_z * rows, rank), bf16),
            jax.ShapeDtypeStruct((hidden, rank), f32),
        ),
        compiler_params=pltpu.CompilerParams(vmem_limit_bytes=16 * mebibyte),
    )(place, *terms, *basis_blocks)


def sum_gradient(local_parts, old_basis, place):
    d_model, hidden = local_parts.shape
    rows = d_model // (2 * n_z)
    blocks = local_parts.reshape(n_z, 2, rows, hidden)
    half = n_z // 2
    arrived = [swap(load_rows(blocks, place, first, True)) for first in (0, half)]
    kept_first, kept_second = [load_rows(blocks, place, first, False) for first in (0, half)]
    basis_own, kept_first = together(old_basis, kept_first)
    basis_up, basis_down = hop(basis_own, basis_own)
    pieces = [list(pair_sum(place, *pair)) for pair in zip((kept_first, kept_second), arrived)]
    basis_up, basis_down, pieces[1][0] = together(basis_up, basis_down, pieces[1][0])
    basis_blocks = [old_basis, basis_up, basis_down]

    long_up = long_down = short_up = short_down = None
    for distance in range(half, 0, -1):
        if distance > 2:
            basis_up, basis_down = hop(basis_up, basis_down)
        elif distance == 2:
            part = old_basis.shape[0] // 2
            basis_up, basis_down = hop(basis_up[:part], basis_down[part:])
        long_up, long_down = hop(
            ring_term(pieces[0][distance], long_up),
            ring_term(pieces[1][-distance], long_down),
        )
        if distance > 1:
            short_up, short_down = hop(
                ring_term(pieces[1][distance - 1], short_up),
                ring_term(pieces[0][1 - distance], short_down),
            )
        if distance > 2:
            long_up, long_down, basis_up, basis_down = together(
                long_up, long_down, basis_up, basis_down
            )
            basis_blocks += [basis_up, basis_down]
        elif distance == 2:
            long_up, long_down = together(long_up, long_down)
            basis_blocks += [basis_up, basis_down]
        if distance > 1:
            short_up, short_down = together(short_up, short_down)
    terms = [pieces[0][0], long_up, short_down, pieces[1][0], short_up, long_down]
    return sum_and_project(place, terms, basis_blocks)


def back_kernel(gradient_ref, sketch_ref, back_ref):
    back_ref[...] = dot_fast(gradient_ref[...], sketch_ref[...], ((1,), (0,)))


def gram_kernel(sketch_ref, gram_ref):
    gram_ref[...] = dot_fast(sketch_ref[...], sketch_ref[...], ((0,), (0,)))


def small_call(kernel, rows, *operands):
    return pl.pallas_call(
        kernel,
        in_specs=[pl.BlockSpec(memory_space=pltpu.VMEM)] * len(operands),
        out_shape=jax.ShapeDtypeStruct((rows, operands[-1].shape[1]), f32),
        compiler_params=pltpu.CompilerParams(vmem_limit_bytes=16 * mebibyte),
        cost_estimate=pl.CostEstimate(flops=2 * 10**9, bytes_accessed=0, transcendentals=0),
    )(*operands)


def sum_blocks(blocks):
    return jnp.sum(blocks.astype(f32), axis=0).astype(bf16)


def spread_z(block):
    copies = jnp.broadcast_to(block[None], (n_z,) + block.shape)
    return lax.all_to_all(copies, "dp", 0, 0, tiled=True, axis_index_groups=z_groups)


def spread_rank(block):
    copies = jnp.broadcast_to(block[None], (lax.axis_size("rank"),) + block.shape)
    return lax.all_to_all(copies, "rank", 0, 0, tiled=True)


def split(values):
    high = values.astype(bf16)
    return high, (values - high.astype(f32)).astype(bf16)


def dot_split(left, right, dims):
    return dot_fast(left[0], right, dims) + dot_fast(left[1], right, dims)


def final_kernel(
    place_ref, inverse_ref, own_cosines_ref, other_cosines_ref, sketch_ref,
    own_moments_ref, other_moments_ref, own_back_ref, other_back_ref,
    basis_ref, moment_ref, second_ref, step_ref,
    first_in, second_in, back_in, update, moment_all, second_all,
):
    z, core = place_ref[0], place_ref[1]
    rank, hidden = first_in.shape
    share_rows = moment_ref.shape[0]
    hidden_own = hidden // (2 * n_z)
    for device_z in range(n_z):
        ring_z = lax.rem(z + (n_z - ring_offsets[device_z]), n_z)
        for side in range(2):
            mine = core == side
            device = ring_z * 2 + side
            rows = pl.ds(pl.multiple_of(device * share_rows, share_rows), share_rows)
            moments = jnp.where(mine, own_moments_ref[device_z], other_moments_ref[device_z])
            first_in[rows] = moments[:share_rows]
            second_in[rows] = moments[share_rows:]
            device = (z ^ flip_order[device_z]) * 2 + side
            rows = pl.ds(pl.multiple_of(device * hidden_own, 8), hidden_own)
            back_in[rows] = jnp.where(
                mine, own_back_ref[device_z].astype(f32), other_back_ref[device_z].astype(f32)
            )
    inverse = inverse_ref[...]
    inverse_split = split(inverse)
    sketch = sketch_ref[...]
    new_basis = (
        dot_fast(sketch, inverse_split[0], ((1,), (1,)))
        + dot_fast(sketch, inverse_split[1], ((1,), (1,)))
    ).astype(bf16)
    basis_ref[...] = new_basis
    cosines = split(own_cosines_ref[...] + other_cosines_ref[...])
    rotation = (
        dot_split(inverse_split, cosines[0], ((1,), (0,)))
        + dot_fast(inverse_split[0], cosines[1], ((1,), (0,)))
    )
    rotation_rounded = rotation.astype(bf16)
    square_rounded = (rotation * rotation).astype(bf16)
    back_images = back_in[...].astype(bf16)
    step = 512
    for low in range(0, rank, step):
        rows = slice(low, low + step)
        projected = dot_split([v[rows] for v in inverse_split], back_images, ((1,), (1,)))
        first_rotated = dot_fast(rotation_rounded[rows], first_in[...], ((1,), (0,)))
        second_rotated = dot_fast(square_rounded[rows], second_in[...], ((1,), (0,)))
        moment_new = beta_one * first_rotated + (1.0 - beta_one) * projected
        second_new = beta_two * second_rotated + (1.0 - beta_two) * projected * projected
        moment_all[rows] = moment_new
        second_all[rows] = second_new
        update[rows] = (moment_new / (jnp.sqrt(second_new) + eps)).astype(bf16)
    own_rows = pl.ds(pl.multiple_of((z * 2 + core) * share_rows, share_rows), share_rows)
    moment_ref[...] = moment_all[own_rows]
    second_ref[...] = second_all[own_rows]
    step_ref[...] = dot_fast(new_basis, update[...], ((1,), (0,))).astype(bf16)


def final_step(place, inverse, cosines, sketch_own, moments, back_images):
    share_rows, hidden = moments[0].shape[1] // 2, moments[0].shape[2]
    rank = inverse.shape[0]
    rows = sketch_own.shape[0]
    in_vmem = pl.BlockSpec(memory_space=pltpu.VMEM)
    return pl.pallas_call(
        final_kernel,
        in_specs=[pl.BlockSpec(memory_space=pltpu.SMEM)] + [in_vmem] * 8,
        out_shape=(
            jax.ShapeDtypeStruct((rows, rank), bf16),
            jax.ShapeDtypeStruct((share_rows, hidden), f32),
            jax.ShapeDtypeStruct((share_rows, hidden), f32),
            jax.ShapeDtypeStruct((rows, hidden), bf16),
        ),
        scratch_shapes=[
            pltpu.VMEM((rank, hidden), bf16),
            pltpu.VMEM((rank, hidden), bf16),
            pltpu.VMEM((hidden, rank), f32),
            pltpu.VMEM((rank, hidden), bf16),
            pltpu.VMEM((rank, hidden), f32),
            pltpu.VMEM((rank, hidden), f32),
        ],
        compiler_params=pltpu.CompilerParams(vmem_limit_bytes=28 * mebibyte),
    )(place, inverse, *cosines, sketch_own, *moments, *back_images)


flip_order = (0, 4, 2, 6, 1, 5, 3, 7)

ring_offsets = (0, 1, 7, 2, 6, 3, 5, 4)


def on_device(grad_parts, old_basis, moment_one, moment_two):
    local_parts = grad_parts[0]
    d_model, hidden_share = local_parts.shape
    share_rows, rank = moment_one.shape[0], old_basis.shape[1]
    basis_rows = old_basis.shape[0]
    own = lax.axis_index("dp")
    z, core = lax.div(own, 2), lax.rem(own, 2)
    n_rank = lax.axis_size("rank")
    hidden_z = hidden_share // n_z
    moments = jnp.concatenate([moment_one, moment_two], axis=0).astype(bf16)

    place = jnp.stack([z, core]).astype(jnp.int32)
    gradient, basis_core, image_part = sum_gradient(local_parts, old_basis, place)
    images = split(image_part + swap(image_part))
    sketch_part = dot_fast(
        jnp.concatenate([gradient, gradient], axis=0), jnp.concatenate(images, axis=0), ((0,), (0,))
    ).astype(bf16)

    rows = d_model // 2 // n_rank
    sketch_part = sum_blocks(
        lax.all_to_all(sketch_part.reshape(n_rank, rows, rank), "rank", 0, 0, tiled=True)
    )
    sketch_rows = sum_blocks(
        lax.all_to_all(
            sketch_part.reshape(n_z, rows // n_z, rank), "dp", 0, 0, tiled=True, axis_index_groups=z_groups
        )
    )
    sketch_rows, moments = together(sketch_rows, moments)
    up = down = moments
    gathered = [moments]
    for distance in range(n_z // 2, 0, -1):
        if distance > 1:
            up, down = hop(up, down)
            up, down = together(up, down)
            gathered += [up, down]
        else:
            gathered.append(lax.ppermute(up, "dp", z_shift(1)))
    moments = jnp.stack(gathered)
    sketch = spread_z(sketch_rows).reshape(rows, rank)
    sketch = spread_rank(sketch).reshape(d_model // 2, rank)
    moments = (moments, swap(moments))

    back_part = small_call(back_kernel, hidden_z, gradient, sketch)
    back_part, sketch = together(back_part, sketch)
    back_part = back_part.reshape(2, hidden_z // 2, rank)
    back_other = swap(pick(back_part, 1 - core))
    gram_part = small_call(gram_kernel, rank, sketch)
    gram_other = swap(gram_part)
    cosine_part = dot_fast(sketch, basis_core, ((0,), (0,)))
    cosine_other = swap(cosine_part)

    back = (pick(back_part, core) + back_other).astype(bf16)[None]
    back, gram_other = together(back, gram_other)
    back = jnp.concatenate([back, lax.ppermute(back, "dp", z_flip(4))])
    *state, token = factor_step(0, gram_part, gram_other)
    for k, distance in ((1, 2), (2, 1)):
        back, token = together(back, token)
        back = jnp.concatenate([back, lax.ppermute(back, "dp", z_flip(distance))])
        *state, token = factor_step(k, *state, token)
    back, token = together(back, token)
    back = (back, swap(back))
    _, inverse, token = factor_step(3, *state, token)

    sketch_own = lax.dynamic_slice_in_dim(sketch, z * basis_rows, basis_rows, 0)
    return final_step(place, inverse, (cosine_part, cosine_other), sketch_own, moments, back)


def solution(mesh):
    in_specs = (P("dp", None, "rank"), P("dp", None), P("dp", "rank"), P("dp", "rank"))
    out_specs = (P("dp", None), P("dp", "rank"), P("dp", "rank"), P("dp", "rank"))
    return jax.shard_map(
        on_device, mesh=mesh, in_specs=in_specs, out_specs=out_specs, check_vma=False
    )
```
